128 devices in a mesh: seq: 16 (over x_hi, y, core), grp: 8 (over z, x_lo).
Axes of the slice: x: 4 (x_hi: 2, x_lo: 2; x = x_hi * 2 + x_lo), y: 4, z: 4, core: 2. Of those that a mesh axis runs over, the one named last changes fastest.
Arguments:
- tile_embeds: bfloat16 [1536, 18432], P('grp', 'seq'), may hold values from -6 to 6
- w_in: bfloat16 [1536, 768], P('grp'), may hold values from -0.15625 to 0.15625
- perturb: bfloat16 [1536, 768], P('grp'), may hold values from -0.078125 to 0.078125
- gain_attn: float32 [768], replicated, may hold values from 0.25 to 1.75
- w_qkv: bfloat16 [768, 2304], replicated, may hold values from -0.25 to 0.25
- temper: float32 [12], replicated, may hold values from 1.5 to 16
- w_out: bfloat16 [768, 768], replicated, may hold values from -0.21875 to 0.21875
- gain_mlp: float32 [768], replicated, may hold values from 0.25 to 1.75
- w_up: bfloat16 [768, 3072], replicated, may hold values from -0.21875 to 0.21875
- w_down: bfloat16 [3072, 768], replicated, may hold values from -0.109375 to 0.109375
Outputs:
- encoded: bfloat16 [18432, 768], P(('seq', 'grp'))
The draws below stay inside these ranges and needn't reach their ends.
All inputs are finite; a program needn't handle non-finite values.
Results may differ from the reference program's by a relative error of at most 0.018.
Values may be sent and summed in bfloat16 or wider, within the bound.
A program may use at most 128 MiB of HBM per device.

```python
import math
import jax
import jax.numpy as jnp
from jax import lax

EMB = 1536
D = 768
HEADS = 12
HEAD = 64
FF = 3072
TOKENS = 18432


def draw_tile_embeds(key, part):
    own_key = jax.random.fold_in(key, 5)
    key_noise = jax.random.fold_in(own_key, 0)
    values = jax.random.normal(key_noise, (EMB, TOKENS), jnp.float32)
    return jnp.clip(values, -6.0, 6.0).astype(jnp.bfloat16)


def draw_w_qkv(key, part):
    own_key = jax.random.fold_in(key, 7)
    entries = jax.random.normal(own_key, (D, 3 * D), jnp.float32) * D ** (-0.5)
    return jnp.clip(entries, -0.25, 0.25).astype(jnp.bfloat16)


def draw_temper(key, part):
    own_key = jax.random.fold_in(key, 11)
    spread = jax.random.uniform(own_key, (HEADS,), jnp.float32)
    lowest = math.log(1.5) + jnp.zeros((HEADS,), jnp.float32)
    highest = math.log(16.0)
    return jnp.exp(lowest + spread * (highest - lowest))


def level_of(rng, shape, pieces, smallest, top_value):
    level = 1.0
    for axis_at, blocks in pieces:
        heights = jax.random.uniform(jax.random.fold_in(jax.random.fold_in(rng, 6), axis_at), (blocks,), jnp.float32, smallest / len(pieces), top_value / len(pieces))
        level = level * jnp.repeat(jnp.exp(heights), shape[axis_at] // blocks).reshape((-1,) + (1,) * (len(shape) - 1 - axis_at))
    return level


def bell_draw(key, extent, deviation, bound, shards=(), dtype=jnp.bfloat16):
    values = deviation * jax.random.normal(key, extent, jnp.float32)
    if shards:
        values = values * level_of(key, extent, shards, -0.22, 0.18)
    return jnp.clip(values, -bound, bound).astype(dtype)


def setup_inputs(seed: int = 0) -> dict:
    splits = jax.random.split(jax.random.key(seed), 11)
    return {
        "tile_embeds": draw_tile_embeds(jax.random.fold_in(splits[10], 71), 0),
        "w_in": bell_draw(splits[1], (EMB, D), EMB ** -0.5, 0.15625, ((0, 8),)),
        "perturb": bell_draw(splits[2], (EMB, D), (4 * EMB) ** -0.5, 0.078125, ((0, 8),)),
        "gain_attn": jnp.clip(1.0 + 0.15 * jax.random.normal(splits[3], (D,), jnp.float32), 0.25, 1.75),
        "w_qkv": draw_w_qkv(jax.random.fold_in(splits[10], 71), 0),
        "temper": draw_temper(jax.random.fold_in(splits[10], 71), 0),
        "w_out": bell_draw(splits[6], (D, D), D ** -0.5, 0.21875),
        "gain_mlp": jnp.clip(1.0 + 0.15 * jax.random.normal(splits[7], (D,), jnp.float32), 0.25, 1.75),
        "w_up": bell_draw(splits[8], (D, FF), D ** -0.5, 0.21875),
        "w_down": bell_draw(splits[9], (FF, D), FF ** -0.5, 0.109375),
    }


def norm_rows(values, gain):
    floats = values.astype(jnp.float32)
    average = lax.optimization_barrier(jnp.mean(floats, axis=-1, keepdims=True))
    centred = floats - average
    spread = lax.optimization_barrier(jnp.mean(centred * centred, axis=-1, keepdims=True))
    return (centred * lax.rsqrt(spread + 1e-05) * gain).astype(jnp.bfloat16)

def reference(tile_embeds, w_in, perturb, gain_attn, w_qkv, temper, w_out, gain_mlp, w_up, w_down):
    w_eff = (w_in.astype(jnp.float32) + perturb.astype(jnp.float32)).astype(jnp.bfloat16)
    hidden = lax.dot_general(tile_embeds, w_eff, (((0,), (0,)), ((), ())), preferred_element_type=jnp.float32).astype(jnp.bfloat16)
    normed_attn = norm_rows(hidden, gain_attn)
    projected = jnp.dot(normed_attn, w_qkv, preferred_element_type=jnp.float32)
    query = projected[:, :D].astype(jnp.bfloat16)
    key_rows = projected[:, D:2 * D].astype(jnp.bfloat16)
    value_rows = projected[:, 2 * D:].astype(jnp.bfloat16)
    keys_float = key_rows.astype(jnp.float32).reshape(TOKENS, HEADS, HEAD)
    values_float = value_rows.astype(jnp.float32).reshape(TOKENS, HEADS, HEAD)
    score_scale = temper * HEAD ** (-0.5)
    block_rows = math.gcd(TOKENS, 512)
    query_blocks = query.astype(jnp.float32).reshape(TOKENS // block_rows, block_rows, HEADS, HEAD)

    def attend(query_block):
        scores = jnp.einsum('qhd,khd->hqk', query_block, keys_float) * score_scale[:, None, None]
        peak = lax.optimization_barrier(jnp.max(scores, axis=-1, keepdims=True))
        expo = jnp.exp(scores - peak)
        totals = lax.optimization_barrier(jnp.sum(expo, axis=-1))
        weights = lax.optimization_barrier(expo.astype(jnp.bfloat16)).astype(jnp.float32)
        summed = jnp.einsum('hqk,khd->qhd', weights, values_float)
        return (summed / jnp.transpose(totals)[:, :, None]).reshape(block_rows, D)
    attended = lax.map(attend, query_blocks).reshape(TOKENS, D).astype(jnp.bfloat16)
    resid = (hidden.astype(jnp.float32) + jnp.dot(attended, w_out, preferred_element_type=jnp.float32)).astype(jnp.bfloat16)
    normed_mlp = norm_rows(resid, gain_mlp)
    activated = jax.nn.gelu(jnp.dot(normed_mlp, w_up, preferred_element_type=jnp.float32)).astype(jnp.bfloat16)
    encoded = resid.astype(jnp.float32) + jnp.dot(activated, w_down, preferred_element_type=jnp.float32)
    return encoded.astype(jnp.bfloat16)
```

```python
import functools

import jax
import jax.numpy as jnp
from jax import lax
from jax.experimental import pallas as pl
from jax.experimental.pallas import tpu as pltpu
from jax.sharding import PartitionSpec as P

MESH = pl.DeviceIdType.MESH
ANY = pl.BlockSpec(memory_space=pl.ANY)
VMEM = pl.BlockSpec(memory_space=pltpu.VMEM)
BF16 = jnp.bfloat16
F32 = jnp.float32
LOG2E = 1.4426950408889634
XS, YS, ZS, CORES = 4, 4, 4, 2
KEY_STEP = 256


def position():
    seq, grp = lax.axis_index("seq"), lax.axis_index("grp")
    x = (seq // 8) * 2 + grp % 2
    return x, (seq // 2) % 4, grp // 2, seq % 2


def device(x, y, z, core):
    return ((x // 2) * 8 + y * 2 + core, z * 2 + x % 2)


def greet(partners):
    barrier = pltpu.get_barrier_semaphore()
    for partner in partners:
        pl.semaphore_signal(barrier, inc=1, device_id=partner, device_id_type=MESH)
    pl.semaphore_wait(barrier, len(partners))


def remote(src, dst, send_sem, recv_sem, partner):
    return pltpu.make_async_remote_copy(
        src_ref=src, dst_ref=dst, send_sem=send_sem, recv_sem=recv_sem,
        device_id=partner, device_id_type=MESH,
    )


def norm_rows(floats, gain):
    average = jnp.mean(floats, axis=-1, keepdims=True)
    centred = floats - average
    spread = jnp.mean(centred * centred, axis=-1, keepdims=True)
    return (centred * lax.rsqrt(spread + 1e-05) * gain).astype(BF16)


def project_kernel(
    embeds_ref, w_in_ref, perturb_ref, gain_ref, w_qkv_ref, scale_ref,
    hidden_ref, q_all, kv_all,
    partial, arrived, q_out, kv_out,
    part_send, part_recv, y_send, y_recv, x_send, x_recv, z_send, z_recv, c_send, c_recv, own_sem,
):
    x, y, z, core = position()
    seq, grp = lax.axis_index("seq"), lax.axis_index("grp")
    groups = 8
    rows = arrived.shape[1]
    width = partial.shape[1]
    ys = [lax.rem(y + d, YS) for d in range(1, YS)]
    xs = [lax.rem(x + d, XS) for d in range(1, XS)]
    zs = [lax.rem(z + d, ZS) for d in range(1, ZS)]
    peers = [(seq, lax.rem(grp + d, groups)) for d in range(1, groups)]
    sibling = device(x, y, z, 1 - core)
    far = [device(lax.rem(x + 2, 4), y, z, core), device(3 - x, y, z, core)]
    greet(peers + [device(x, there, z, core) for there in ys] + [sibling] + far)

    w_eff = (w_in_ref[...].astype(F32) + perturb_ref[...].astype(F32)).astype(BF16)
    for at in range(0, partial.shape[0], 128):
        partial[at : at + 128, :] = lax.dot_general(
            embeds_ref[:, at : at + 128], w_eff, (((0,), (0,)), ((), ())),
            preferred_element_type=F32,
        ).astype(BF16)
    sums = []
    for d in range(1, groups):
        there = lax.rem(grp + d, groups)
        start = pl.multiple_of(there * rows, 16)
        sums.append(remote(
            partial.at[pl.ds(start, rows)], arrived.at[d - 1],
            part_send.at[d - 1], part_recv.at[d - 1], (seq, there),
        ))
        sums[-1].start()
    total = partial[pl.ds(pl.multiple_of(grp * rows, 16), rows), :].astype(F32)
    for d in range(1, groups):
        sums[d - 1].wait_recv()
        total = total + arrived[d - 1].astype(F32)
    hidden = total.astype(BF16)
    hidden_ref[...] = hidden
    normed = norm_rows(hidden.astype(F32), gain_ref[...])

    share = width // YS
    keys = jnp.dot(normed, w_qkv_ref[:, width : 2 * width], preferred_element_type=F32)
    values = jnp.dot(normed, w_qkv_ref[:, 2 * width :], preferred_element_type=F32)
    for part in range(YS):
        cols = slice(part * share, (part + 1) * share)
        kv_out[part] = jnp.concatenate([keys[:, cols], values[:, cols]], axis=1).astype(BF16)
    kv_copies = []
    for i, there in enumerate(ys):
        kv_copies.append(remote(
            kv_out.at[there], kv_all.at[z, core, y], y_send.at[0, i], y_recv.at[0, i],
            device(x, there, z, core),
        ))
        kv_copies[-1].start()
    own_kv = pltpu.make_async_copy(kv_out.at[y], kv_all.at[z, core, y], own_sem.at[0])
    own_kv.start()
    query = jnp.dot(normed, w_qkv_ref[:, :width], preferred_element_type=F32) * scale_ref[...]
    blank = jnp.zeros((rows, q_out.shape[2] - share), F32)
    for part in range(YS):
        cols = slice(part * share, (part + 1) * share)
        q_out[part] = jnp.concatenate([query[:, cols], blank], axis=1).astype(BF16)
    q_copies = []
    for i, there in enumerate(ys):
        q_copies.append(remote(
            q_out.at[there], q_all.at[x, y], y_send.at[1, i], y_recv.at[1, i],
            device(x, there, z, core),
        ))
        q_copies[-1].start()
    own_q = pltpu.make_async_copy(q_out.at[y], q_all.at[x, y], own_sem.at[1])
    own_q.start()

    own_kv.wait()
    for copy in kv_copies:
        copy.wait_recv()
    block = kv_all.at[z, core]
    z_copies = []
    for i, there in enumerate(zs):
        z_copies.append(remote(
            block, block, z_send.at[i], z_recv.at[i], device(x, y, there, core)
        ))
        z_copies[-1].start()
    c_copies = [remote(block, block, c_send.at[0], c_recv.at[0], sibling)]
    c_copies[0].start()

    own_q.wait()
    for copy in q_copies:
        copy.wait_recv()
    x_copies = []
    for i, there in enumerate(xs):
        x_copies.append(remote(
            q_all.at[x], q_all.at[x], x_send.at[i], x_recv.at[i], device(there, y, z, core)
        ))
        x_copies[-1].start()
    for i in range(ZS - 1):
        z_copies[i].wait_recv()
        came = kv_all.at[lax.rem(z + ZS - 1 - i, ZS), core]
        c_copies.append(remote(came, came, c_send.at[i + 1], c_recv.at[i + 1], sibling))
        c_copies[-1].start()
    for copy in x_copies + c_copies:
        copy.wait_recv()
    for copy in sums + kv_copies + q_copies + z_copies + c_copies + x_copies:
        copy.wait_send()


def place(head):
    return divmod(head, 2)


def attend_kernel(q_ref, kv_ref, o_ref, acc_ref):
    rows, total = q_ref.shape[0], kv_ref.shape[0]
    heads, size = 3, 64
    lane = lax.broadcasted_iota(jnp.int32, (rows, 128), 1)
    ones = jnp.ones((KEY_STEP, 128), BF16)
    tops = jnp.ones((8, KEY_STEP), BF16)
    sample_step = total // (KEY_STEP // 16)
    for head in range(heads):
        q_tile, q_half = place(head)
        v_tile, v_half = place(head + heads)
        q_cols = slice(q_tile * 128, (q_tile + 1) * 128)
        v_cols = slice(v_tile * 128, (v_tile + 1) * 128)
        query = jnp.where(lane // size == q_half, q_ref[:, q_cols], jnp.zeros((), BF16))
        q_turned = query.T
        sample = jnp.concatenate(
            [kv_ref[at : at + 16, q_cols] for at in range(0, total, sample_step)], axis=0
        )
        level = jnp.max(
            jnp.dot(sample, q_turned, preferred_element_type=F32), axis=0, keepdims=True
        ).astype(BF16)
        row = lax.broadcasted_iota(jnp.int32, (128, rows), 0)
        shift = jnp.where(row == 0, jnp.broadcast_to(-level, (128, rows)), jnp.zeros((), BF16))
        q_full = jnp.concatenate([q_turned, shift], axis=0)
        acc = jnp.zeros((136, rows), F32)
        for at in range(0, total, KEY_STEP):
            keys = jnp.concatenate([kv_ref[at : at + KEY_STEP, q_cols], ones], axis=1)
            scores = jnp.dot(keys, q_full, preferred_element_type=F32)
            weights = jnp.exp2(scores).astype(BF16)
            values = jnp.concatenate([kv_ref[at : at + KEY_STEP, v_cols].T, tops], axis=0)
            acc = acc + jnp.dot(values, weights, preferred_element_type=F32)
        acc_ref[0:136] = acc
        acc_ref[136:144] = jnp.broadcast_to(level.astype(F32), (8, rows))
        sums = acc[128:129]
        good = (sums > 2.0**-100) & (sums < 2.0**100)
        bad = jnp.max(jnp.where(good, 0.0, 1.0))

        @pl.when(bad > 0.5)
        def _():
            def step(i, carry):
                peak, kept = carry
                at = pl.multiple_of(i * KEY_STEP, KEY_STEP)
                scores = jnp.dot(
                    kv_ref[pl.ds(at, KEY_STEP), q_cols], q_turned, preferred_element_type=F32
                )
                higher = jnp.maximum(peak, jnp.max(scores, axis=0, keepdims=True))
                weights = jnp.exp2(scores - higher).astype(BF16)
                values = jnp.concatenate(
                    [kv_ref[pl.ds(at, KEY_STEP), v_cols].T, tops], axis=0
                )
                kept = kept * jnp.exp2(peak - higher) + jnp.dot(
                    values, weights, preferred_element_type=F32
                )
                return higher, kept

            peak, kept = lax.fori_loop(
                0, total // KEY_STEP, step,
                (jnp.full((1, rows), -jnp.inf, F32), jnp.zeros((136, rows), F32)),
            )
            acc_ref[0:136] = kept
            acc_ref[136:144] = jnp.broadcast_to(peak, (8, rows))

        sums = acc_ref[128:129]
        inverse = 1.0 / sums
        log_sum = acc_ref[136:137] + jnp.log2(sums)
        high = log_sum.astype(BF16).astype(F32)
        acc_ref[144 + head * 64 : 208 + head * 64] = (
            acc_ref[v_half * size : (v_half + 1) * size] * inverse
        )
        acc_ref[336 + head * 16 : 344 + head * 16] = jnp.broadcast_to(high, (8, rows))
        acc_ref[344 + head * 16 : 352 + head * 16] = jnp.broadcast_to(log_sum - high, (8, rows))
    acc_ref[384:400] = jnp.zeros((16, rows), F32)
    for at in range(0, rows, 128):
        for tile in range(2):
            o_ref[at : at + 128, tile * 128 : (tile + 1) * 128] = (
                acc_ref[144 + tile * 128 : 272 + tile * 128, at : at + 128].T.astype(BF16)
            )


def finish_kernel(
    o_ref, hidden_ref, w_out_ref, gain_ref, w_up_ref, w_down_ref,
    out_ref,
    parts, mine, turned, up, down,
    x_send, x_recv, y_send, y_recv, w_sem,
):
    x, y, z, core = position()
    ys = [lax.rem(y + d, YS) for d in range(1, YS)]
    xs = [lax.rem(x + d, XS) for d in range(1, XS)]
    loads = [
        pltpu.make_async_copy(w_up_ref, up, w_sem.at[0]),
        pltpu.make_async_copy(w_down_ref, down, w_sem.at[1]),
    ]
    for load in loads:
        load.start()
    greet([device(x, there, z, core) for there in ys] + [device(there, y, z, core) for there in xs])
    x_copies = []
    for i, there in enumerate(xs):
        x_copies.append(remote(
            o_ref.at[there], parts.at[i], x_send.at[i], x_recv.at[i], device(there, y, z, core)
        ))
        x_copies[-1].start()
    for copy in x_copies:
        copy.wait_recv()
    rows = hidden_ref.shape[0]
    heads, size = 3, 64
    tops = 192
    for block in range(YS):
        pieces = [o_ref[x, block].astype(F32)] + [parts[i, block].astype(F32) for i in range(XS - 1)]
        merged = []
        for head in range(heads):
            at = tops + head * 16
            logs = [piece[:, at : at + 1] + piece[:, at + 8 : at + 9] for piece in pieces]
            peak = functools.reduce(jnp.maximum, logs)
            shares = [jnp.exp2(log - peak) for log in logs]
            inverse = 1.0 / functools.reduce(jnp.add, shares)
            cols = slice(head * size, (head + 1) * size)
            merged.append(functools.reduce(
                jnp.add, [piece[:, cols] * (one * inverse) for piece, one in zip(pieces, shares)]
            ))
        merged.append(jnp.zeros((rows, 64), F32))
        mine[block] = jnp.concatenate(merged, axis=1).astype(BF16)
    y_copies = []
    for i, there in enumerate(ys):
        y_copies.append(remote(
            mine.at[there], turned.at[y], y_send.at[i], y_recv.at[i], device(x, there, z, core)
        ))
        y_copies[-1].start()
    turned[y] = mine[y]
    for copy in y_copies:
        copy.wait_recv()
    share = heads * size
    mixed = hidden_ref[...].astype(F32)
    for part in range(YS):
        mixed = mixed + jnp.dot(
            turned[part][:, :share], w_out_ref[part * share : (part + 1) * share, :],
            preferred_element_type=F32,
        )
    resid = mixed.astype(BF16).astype(F32)
    normed = norm_rows(resid, gain_ref[...])
    loads[0].wait()
    loads[1].wait()
    encoded = resid
    step = 768
    for at in range(0, up.shape[1], step):
        raised = jnp.dot(normed, up[:, at : at + step], preferred_element_type=F32)
        active = jax.nn.gelu(raised).astype(BF16)
        encoded = encoded + jnp.dot(active, down[at : at + step, :], preferred_element_type=F32)
    out_ref[...] = encoded.astype(BF16)
    for copy in x_copies + y_copies:
        copy.wait_send()


def on_device(tile_embeds, w_in, perturb, gain_attn, w_qkv, temper, w_out, gain_mlp, w_up, w_down):
    width = w_qkv.shape[0]
    rows = tile_embeds.shape[1] // 8
    size = width // temper.shape[0]
    scale = jnp.repeat(temper * (size ** (-0.5) * LOG2E), size)[None, :]
    dma = pltpu.SemaphoreType.DMA
    hidden, q_all, kv_all = pl.pallas_call(
        project_kernel,
        out_shape=(
            jax.ShapeDtypeStruct((rows, width), BF16),
            jax.ShapeDtypeStruct((XS, YS, rows, 256), BF16),
            jax.ShapeDtypeStruct((ZS, CORES, YS, rows, 384), BF16),
        ),
        in_specs=[VMEM] * 6,
        out_specs=(VMEM, ANY, ANY),
        scratch_shapes=[
            pltpu.VMEM((8 * rows, width), BF16),
            pltpu.VMEM((7, rows, width), BF16),
            pltpu.VMEM((YS, rows, 256), BF16),
            pltpu.VMEM((YS, rows, 384), BF16),
            dma((7,)), dma((7,)), dma((2, 3)), dma((2, 3)), dma((3,)), dma((3,)),
            dma((3,)), dma((3,)), dma((4,)), dma((4,)), dma((2,)),
        ],
        compiler_params=pltpu.CompilerParams(
            collective_id=0, has_side_effects=True, vmem_limit_bytes=40 * 2**20
        ),
        name="project",
    )(tile_embeds, w_in, perturb, gain_attn[None, :], w_qkv, scale)
    q_rows, kv_rows = XS * YS * rows, ZS * CORES * YS * rows
    parts = pl.pallas_call(
        attend_kernel,
        out_shape=jax.ShapeDtypeStruct((q_rows, 256), BF16),
        in_specs=[VMEM, VMEM],
        out_specs=VMEM,
        scratch_shapes=[pltpu.VMEM((400, q_rows), F32)],
        compiler_params=pltpu.CompilerParams(vmem_limit_bytes=56 * 2**20),
        name="attend",
    )(q_all.reshape(q_rows, 256), kv_all.reshape(kv_rows, 384))
    return pl.pallas_call(
        finish_kernel,
        out_shape=jax.ShapeDtypeStruct((rows, width), BF16),
        in_specs=[VMEM, VMEM, VMEM, VMEM, ANY, ANY],
        out_specs=VMEM,
        scratch_shapes=[
            pltpu.VMEM((XS - 1, YS, rows, 256), BF16),
            pltpu.VMEM((YS, rows, 256), BF16),
            pltpu.VMEM((YS, rows, 256), BF16),
            pltpu.VMEM(w_up.shape, BF16),
            pltpu.VMEM(w_down.shape, BF16),
            dma((3,)), dma((3,)), dma((3,)), dma((3,)), dma((2,)),
        ],
        compiler_params=pltpu.CompilerParams(
            collective_id=1, has_side_effects=True, vmem_limit_bytes=40 * 2**20
        ),
        name="finish",
    )(parts.reshape(XS, YS, rows, 256), hidden, w_out, gain_mlp[None, :], w_up, w_down)


def solution(mesh):
    placed = (P("grp", "seq"), P("grp", None), P("grp", None), P(), P(), P(), P(), P(), P(), P())
    return jax.shard_map(
        on_device, mesh=mesh, in_specs=placed, out_specs=P(("seq", "grp"), None), check_vma=False
    )
```

```python
import functools

import jax
import jax.numpy as jnp
from jax import lax
from jax.experimental import pallas as pl
from jax.experimental.pallas import tpu as pltpu
from jax.sharding import PartitionSpec as P

MESH = pl.DeviceIdType.MESH
ANY = pl.BlockSpec(memory_space=pl.ANY)
VMEM = pl.BlockSpec(memory_space=pltpu.VMEM)
SMEM = pl.BlockSpec(memory_space=pltpu.SMEM)
BF16 = jnp.bfloat16
F32 = jnp.float32
LOG2E = 1.4426950408889634
SIDE = 4
GROUPS = 8
TEAM = 3
SIZE = 64
SHARE = TEAM * SIZE
LANES = 128
SLOTS = 8
FORWARD = {0: 1, 2: 4, 3: 5, 6: 7}
Z_SLOT = {1: 2, 3: 3, 2: 6}


def position():
    seq, grp = lax.axis_index("seq"), lax.axis_index("grp")
    x = (seq // 8) * 2 + grp % 2
    return x, (seq // 2) % 4, grp // 2, seq % 2


def device(x, y, z, core):
    return ((x // 2) * 8 + y * 2 + core, z * 2 + x % 2)


def remote(src, dst, send_sem, recv_sem, partner):
    return pltpu.make_async_remote_copy(
        src_ref=src, dst_ref=dst, send_sem=send_sem, recv_sem=recv_sem,
        device_id=partner, device_id_type=MESH,
    )


def norm_rows(floats, gain):
    average = jnp.mean(floats, axis=-1, keepdims=True)
    centred = floats - average
    spread = jnp.mean(centred * centred, axis=-1, keepdims=True)
    return (centred * lax.rsqrt(spread + 1e-05) * gain).astype(BF16)


def layer_kernel(
    embeds_hbm, w_in_hbm, perturb_hbm, gain_attn, w_qkv_hbm, temper, w_out_hbm, gain_mlp,
    w_up_hbm, w_down_hbm,
    out_ref,
    embeds, w_in, perturb, w_qkv, w_out, w_up, w_down,
    partial, arrived, q_out, kv_out, q_all, kv_all,
    turned, score_a, score_b, acc, peak, o_out, o_in, mine, back,
    load_sem, part_send, part_recv, y_send, y_recv, x_send, x_recv, z_send, kv_recv, c_send,
    o_send, o_recv, b_send, b_recv,
):
    x, y, z, core = position()
    seq, grp = lax.axis_index("seq"), lax.axis_index("grp")
    rows, width = out_ref.shape
    block = SIDE * rows
    ahead = (1, 2, 3)
    x_to = {d: device(lax.rem(x + d, SIDE), y, z, core) for d in ahead}
    y_to = {d: device(x, lax.rem(y + d, SIDE), z, core) for d in ahead}
    z_to = {d: device(x, y, lax.rem(z + d, SIDE), core) for d in ahead}
    sibling = device(x, y, z, 1 - core)
    peers = [(seq, lax.rem(grp + d, GROUPS)) for d in range(1, GROUPS)]
    far = [device(lax.rem(x + 2, SIDE), y, z, core), device(3 - x, y, z, core)]

    loads = [
        pltpu.make_async_copy(src, dst, load_sem.at[i])
        for i, (src, dst) in enumerate([
            (embeds_hbm, embeds), (w_in_hbm, w_in), (perturb_hbm, perturb), (w_qkv_hbm, w_qkv),
            (w_out_hbm, w_out), (w_up_hbm, w_up), (w_down_hbm, w_down),
        ])
    ]
    for load in loads:
        load.start()
    barrier = pltpu.get_barrier_semaphore()
    greeted = peers + [y_to[d] for d in ahead] + [sibling] + far
    for partner in greeted:
        pl.semaphore_signal(barrier, inc=1, device_id=partner, device_id_type=MESH)
    for load in loads[:3]:
        load.wait()
    w_eff = (w_in[...].astype(F32) + perturb[...].astype(F32)).astype(BF16)
    for at in range(0, partial.shape[0], LANES):
        partial[at : at + LANES, :] = lax.dot_general(
            embeds[:, at : at + LANES], w_eff, (((0,), (0,)), ((), ())),
            preferred_element_type=F32,
        ).astype(BF16)
    pl.semaphore_wait(barrier, len(greeted))

    copies = []

    def send(*args):
        copy = remote(*args)
        copy.start()
        copies.append(copy)
        return copy

    sums = {}
    for d in (1, 2, 3, 4, 5, 6, 7):
        there = lax.rem(grp + d, GROUPS)
        start = pl.multiple_of(there * rows, 16)
        sums[d] = send(
            partial.at[pl.ds(start, rows)], arrived.at[d - 1],
            part_send.at[d - 1], part_recv.at[d - 1], (seq, there),
        )
    total = partial[pl.ds(pl.multiple_of(grp * rows, 16), rows), :].astype(F32)
    for d in range(1, GROUPS):
        sums[d].wait_recv()
        total = total + arrived[d - 1].astype(F32)
    hidden = total.astype(BF16).astype(F32)
    normed = norm_rows(hidden, gain_attn[...][None, :])

    loads[3].wait()
    keys = jnp.dot(normed, w_qkv[:, width : 2 * width], preferred_element_type=F32)
    values = jnp.dot(normed, w_qkv[:, 2 * width :], preferred_element_type=F32)
    kv_y = {}
    q_y = {}

    def exchange_kv(head):
        for part in range(SIDE):
            at = part * SHARE + head * SIZE
            kv_out[head, part] = jnp.concatenate(
                [keys[:, at : at + SIZE], values[:, at : at + SIZE]], axis=1
            ).astype(BF16)
        for d in ahead:
            kv_y[head, d] = send(
                kv_out.at[head, lax.rem(y + d, SIDE)], kv_all.at[head, 0, pl.ds(d * rows, rows)],
                y_send.at[head, d - 1], y_recv.at[head, d - 1], y_to[d],
            )
        kv_all[head, 0, 0:rows] = kv_out[head, y]

    def exchange_q(tile):
        for part in range(SIDE):
            pieces = []
            for head in (2 * tile, 2 * tile + 1):
                if head < TEAM:
                    at = part * SHARE + head * SIZE
                    pieces.append(
                        query[:, at : at + SIZE]
                        * (temper[part * TEAM + head] * (SIZE ** (-0.5) * LOG2E))
                    )
                else:
                    pieces.append(jnp.zeros((rows, SIZE), F32))
            q_out[tile, part] = jnp.concatenate(pieces, axis=1).astype(BF16)
        for d in ahead:
            q_y[tile, d] = send(
                q_out.at[tile, lax.rem(y + d, SIDE)], q_all.at[tile, 0, pl.ds(d * rows, rows)],
                y_send.at[TEAM + tile, d - 1], y_recv.at[TEAM + tile, d - 1], y_to[d],
            )
        q_all[tile, 0, 0:rows] = q_out[tile, y]

    exchange_kv(0)
    query = jnp.dot(normed, w_qkv[:, :width], preferred_element_type=F32)
    exchange_q(0)
    exchange_kv(1)
    exchange_kv(2)
    exchange_q(1)

    kv_z = {}
    kv_c = {}
    q_x = {}

    def spread_kv(head):
        for d in ahead:
            kv_y[head, d].wait_recv()
        own = kv_all.at[head, 0]
        for d in (1, 3, 2):
            kv_z[head, Z_SLOT[d]] = send(
                own, kv_all.at[head, Z_SLOT[d]], z_send.at[head, d - 1],
                kv_recv.at[head, Z_SLOT[d]], z_to[d],
            )
        forward_kv(head, 0)

    def forward_kv(head, slot):
        to = FORWARD[slot]
        kv_c[head, to] = remote(
            kv_all.at[head, slot], kv_all.at[head, to], c_send.at[head, to],
            kv_recv.at[head, to], sibling,
        )
        kv_c[head, to].start()

    def spread_q(tile):
        for d in ahead:
            q_y[tile, d].wait_recv()
        for d in (1, 3, 2):
            q_x[tile, d] = send(
                q_all.at[tile, 0], q_all.at[tile, d], x_send.at[tile, d - 1],
                x_recv.at[tile, d - 1], x_to[d],
            )

    spread_kv(0)
    spread_q(0)
    spread_kv(1)
    spread_kv(2)
    spread_q(1)

    columns = turned.shape[1]
    ones = jnp.ones((8, block), BF16)
    o_x = {}
    for head in range(TEAM):
        tile, half = divmod(head, 2)
        if half == 0:
            for d in ahead:
                q_x[tile, d].wait_recv()
        for slot in range(SIDE):
            part = q_all[tile, slot].T
            turned[0:SIZE, slot * block : (slot + 1) * block] = part[half * SIZE : (half + 1) * SIZE]
        turned[SIZE:LANES, :] = jnp.zeros((LANES - SIZE, columns), BF16)
        acc[...] = jnp.zeros(acc.shape, F32)
        peak[...] = jnp.full(peak.shape, -1e30, F32)

        def score(slot, into, head=head):
            into[...] = jnp.dot(kv_all[head, slot], turned[...], preferred_element_type=F32)

        def absorb(slot, scores_ref, head=head):
            scores = scores_ref[...]
            before = peak[0:1, :]
            after = jnp.maximum(before, jnp.max(scores, axis=0, keepdims=True))
            peak[0:1, :] = after
            weights = jnp.exp2(scores - after).astype(BF16)
            both = kv_all[head, slot].T
            values = jnp.concatenate([both[SIZE:], ones], axis=0)
            acc[...] = acc[...] * jnp.exp2(before - after) + jnp.dot(
                values, weights, preferred_element_type=F32
            )

        def wait_slot(slot, head=head):
            pltpu.make_async_copy(
                kv_all.at[head, slot], kv_all.at[head, slot], kv_recv.at[head, slot]
            ).wait()

        score(0, score_a)

        def pair(step, _, head=head):
            @pl.when(step == 0)
            def _():
                wait_slot(2)
                forward_kv(head, 2)
                wait_slot(1)

            @pl.when(step == 1)
            def _():
                wait_slot(3)
                forward_kv(head, 3)
                wait_slot(4)

            @pl.when(step == 2)
            def _():
                wait_slot(6)
                forward_kv(head, 6)
                wait_slot(5)

            @pl.when(step == 3)
            def _():
                wait_slot(7)

            score(2 * step + 1, score_b)
            absorb(2 * step, score_a)
            score(jnp.minimum(2 * step + 2, SLOTS - 1), score_a)
            absorb(2 * step + 1, score_b)
            return 0

        lax.fori_loop(0, SLOTS // 2, pair, 0)

        sums_row = acc[SIZE : SIZE + 1, :]
        log_sum = peak[0:1, :] + jnp.log2(sums_row)
        high = log_sum.astype(BF16).astype(F32)
        low = log_sum - high
        whole = jnp.concatenate(
            [
                acc[0:SIZE, :] * (1.0 / sums_row),
                jnp.broadcast_to(high, (8, columns)),
                jnp.broadcast_to(low, (8, columns)),
                jnp.zeros((LANES - SIZE - 16, columns), F32),
            ],
            axis=0,
        )
        for slot in (1, 3, 2, 0):
            o_out[head, slot] = whole[:, slot * block : (slot + 1) * block].T.astype(BF16)
            if slot:
                o_x[head, slot] = send(
                    o_out.at[head, slot], o_in.at[head, slot - 1], o_send.at[head, slot - 1],
                    o_recv.at[head, slot - 1], x_to[SIDE - slot],
                )

    def merge(head):
        for slot in ahead:
            o_x[head, slot].wait_recv()
        pieces = [o_out[head, 0].astype(F32)]
        pieces += [o_in[head, slot - 1].astype(F32) for slot in ahead]
        logs = [piece[:, SIZE : SIZE + 1] + piece[:, SIZE + 8 : SIZE + 9] for piece in pieces]
        top = functools.reduce(jnp.maximum, logs)
        shares = [jnp.exp2(log - top) for log in logs]
        inverse = 1.0 / functools.reduce(jnp.add, shares)
        return functools.reduce(
            jnp.add,
            [piece[:, :SIZE] * (one * inverse) for piece, one in zip(pieces, shares)],
        )

    b_y = {}

    def give_back(tile, value):
        mine[tile] = value.astype(BF16)
        for d in ahead:
            b_y[tile, d] = send(
                mine.at[tile, pl.ds(d * rows, rows)], back.at[tile, d],
                b_send.at[tile, d - 1], b_recv.at[tile, d - 1], y_to[SIDE - d],
            )

    give_back(0, jnp.concatenate([merge(0), merge(1)], axis=1))
    give_back(1, jnp.concatenate([merge(2), jnp.zeros((block, SIZE), F32)], axis=1))
    mixed = hidden
    loads[4].wait()
    for tile in range(2):
        used = LANES if tile == 0 else SIZE
        for d in range(SIDE):
            if d:
                b_y[tile, d].wait_recv()
                piece = back[tile, d]
            else:
                piece = mine[tile, 0:rows]
            owner = lax.rem(y + d, SIDE)
            start = pl.multiple_of(owner * SHARE + tile * LANES, 16)
            mixed = mixed + jnp.dot(
                piece[:, :used], w_out[pl.ds(start, used), :], preferred_element_type=F32
            )
    resid = mixed.astype(BF16).astype(F32)
    normed = norm_rows(resid, gain_mlp[...][None, :])
    loads[5].wait()
    loads[6].wait()
    encoded = resid
    for at in range(0, w_up.shape[1], width):
        raised = jnp.dot(normed, w_up[:, at : at + width], preferred_element_type=F32)
        active = jax.nn.gelu(raised).astype(BF16)
        encoded = encoded + jnp.dot(active, w_down[at : at + width, :], preferred_element_type=F32)
    out_ref[...] = encoded.astype(BF16)
    for copy in copies:
        copy.wait_send()
    for head in range(TEAM):
        for slot, to in FORWARD.items():
            pltpu.make_async_copy(
                kv_all.at[head, slot], kv_all.at[head, slot], c_send.at[head, to]
            ).wait()


def on_device(tile_embeds, w_in, perturb, gain_attn, w_qkv, temper, w_out, gain_mlp, w_up, w_down):
    width = w_qkv.shape[0]
    rows = tile_embeds.shape[1] // GROUPS
    block = SIDE * rows
    columns = SIDE * block
    dma = pltpu.SemaphoreType.DMA
    vmem = pltpu.VMEM
    return pl.pallas_call(
        layer_kernel,
        out_shape=jax.ShapeDtypeStruct((rows, width), BF16),
        in_specs=[ANY, ANY, ANY, VMEM, ANY, SMEM, ANY, VMEM, ANY, ANY],
        out_specs=VMEM,
        scratch_shapes=[
            vmem(tile_embeds.shape, BF16), vmem(w_in.shape, BF16), vmem(perturb.shape, BF16),
            vmem(w_qkv.shape, BF16), vmem(w_out.shape, BF16), vmem(w_up.shape, BF16),
            vmem(w_down.shape, BF16),
            vmem((GROUPS * rows, width), BF16),
            vmem((GROUPS - 1, rows, width), BF16),
            vmem((2, SIDE, rows, LANES), BF16),
            vmem((TEAM, SIDE, rows, LANES), BF16),
            vmem((2, SIDE, block, LANES), BF16),
            vmem((TEAM, SLOTS, block, LANES), BF16),
            vmem((LANES, columns), BF16),
            vmem((block, columns), F32),
            vmem((block, columns), F32),
            vmem((SIZE + 8, columns), F32),
            vmem((8, columns), F32),
            vmem((TEAM, SIDE, block, LANES), BF16),
            vmem((TEAM, SIDE - 1, block, LANES), BF16),
            vmem((2, block, LANES), BF16),
            vmem((2, SIDE, rows, LANES), BF16),
            dma((7,)), dma((7,)), dma((7,)), dma((5, 3)), dma((5, 3)), dma((2, 3)), dma((2, 3)),
            dma((TEAM, 3)), dma((TEAM, SLOTS)), dma((TEAM, SLOTS)),
            dma((TEAM, 3)), dma((TEAM, 3)), dma((2, 3)), dma((2, 3)),
        ],
        compiler_params=pltpu.CompilerParams(
            collective_id=0, has_side_effects=True, vmem_limit_bytes=56 * 2**20
        ),
        name="layer",
    )(tile_embeds, w_in, perturb, gain_attn, w_qkv, temper, w_out, gain_mlp, w_up, w_down)


def solution(mesh):
    placed = (P("grp", "seq"), P("grp", None), P("grp", None), P(), P(), P(), P(), P(), P(), P())
    return jax.shard_map(
        on_device, mesh=mesh, in_specs=placed, out_specs=P(("seq", "grp"), None), check_vma=False
    )
```

```python
import functools

import jax
import jax.numpy as jnp
from jax import lax
from jax.experimental import pallas as pl
from jax.experimental.pallas import tpu as pltpu
from jax.sharding import PartitionSpec as P

MESH = pl.DeviceIdType.MESH
ANY = pl.BlockSpec(memory_space=pl.ANY)
VMEM = pl.BlockSpec(memory_space=pltpu.VMEM)
SMEM = pl.BlockSpec(memory_space=pltpu.SMEM)
BF16 = jnp.bfloat16
F32 = jnp.float32
LOG2E = 1.4426950408889634
SIDE = 4
GROUPS = 8
TEAM = 3
SIZE = 64
SHARE = TEAM * SIZE
LANES = 128
SLOTS = 8
FOLD = 80
STRIP = 256
FORWARD = {0: 1, 2: 4, 3: 5, 6: 7}
Z_SLOT = {1: 2, 3: 3, 2: 6}


def position():
    seq, grp = lax.axis_index("seq"), lax.axis_index("grp")
    x = (seq // 8) * 2 + grp % 2
    return x, (seq // 2) % 4, grp // 2, seq % 2


def device(x, y, z, core):
    return ((x // 2) * 8 + y * 2 + core, z * 2 + x % 2)


def remote(src, dst, send_sem, recv_sem, partner):
    return pltpu.make_async_remote_copy(
        src_ref=src, dst_ref=dst, send_sem=send_sem, recv_sem=recv_sem,
        device_id=partner, device_id_type=MESH,
    )


def fold(piece):
    rows = piece.shape[0]
    blank = jnp.zeros((2 * FOLD - rows, SIZE), piece.dtype)
    lower = jnp.concatenate([piece[FOLD:], blank], axis=0)
    return jnp.concatenate([piece[:FOLD], lower], axis=1).astype(BF16)


def unfold(folded, rows):
    pieces = []
    for at in range(0, folded.shape[0], FOLD):
        pieces += [folded[at : at + FOLD, :SIZE], folded[at : at + rows - FOLD, SIZE:]]
    return jnp.concatenate(pieces, axis=0)


def norm_rows(floats, gain):
    average = jnp.mean(floats, axis=-1, keepdims=True)
    centred = floats - average
    spread = jnp.mean(centred * centred, axis=-1, keepdims=True)
    return (centred * lax.rsqrt(spread + 1e-05) * gain).astype(BF16)


def layer_kernel(
    embeds_hbm, w_in_hbm, perturb_hbm, gain_attn, w_qkv_hbm, temper, w_out_hbm, gain_mlp,
    w_up_hbm, w_down_hbm,
    out_ref,
    embeds, w_in, perturb, w_qkv, w_out, w_up, w_down,
    w_all, embed_out, embed_all, partial, arrived, q_out, kv_out, q_all, kv_all,
    turned, score_a, score_b, acc, peak, o_out, o_in, l_out, l_in, mine, back,
    load_sem, w_send, w_recv, e_send, e_recv, part_send, part_recv, y_send, y_recv, x_send, x_recv, z_send, kv_recv, c_send,
    o_send, o_recv, b_send, b_recv,
):
    x, y, z, core = position()
    rows, width = out_ref.shape
    block = SIDE * rows
    ahead = (1, 2, 3)
    x_to = {d: device(lax.rem(x + d, SIDE), y, z, core) for d in ahead}
    y_to = {d: device(x, lax.rem(y + d, SIDE), z, core) for d in ahead}
    z_to = {d: device(x, y, lax.rem(z + d, SIDE), core) for d in ahead}
    sibling = device(x, y, z, 1 - core)
    loads = [
        pltpu.make_async_copy(src, dst, load_sem.at[i])
        for i, (src, dst) in enumerate([
            (embeds_hbm, embeds), (w_in_hbm, w_in), (perturb_hbm, perturb), (w_qkv_hbm, w_qkv),
            (w_out_hbm, w_out), (w_up_hbm, w_up), (w_down_hbm, w_down),
        ])
    ]
    for load in loads:
        load.start()
    barrier = pltpu.get_barrier_semaphore()
    greeted = [to[d] for to in (x_to, y_to, z_to) for d in ahead] + [sibling]
    for partner in greeted:
        pl.semaphore_signal(barrier, inc=1, device_id=partner, device_id_type=MESH)
    copies = []

    def send(*args):
        copy = remote(*args)
        copy.start()
        copies.append(copy)
        return copy

    for load in loads[1:3]:
        load.wait()
    half = width // 2
    w_eff = (w_in[...].astype(F32) + perturb[...].astype(F32)).astype(BF16)
    for side in range(2):
        w_all[0, side] = w_eff[:, side * half : (side + 1) * half]
    pl.semaphore_wait(barrier, len(greeted))
    w_z, w_c = {}, {}
    for d in (1, 3, 2):
        w_z[d] = send(
            w_all.at[0, core], w_all.at[d, core], w_send.at[d - 1], w_recv.at[d - 1], z_to[d]
        )
    loads[0].wait()
    pair = 2 * rows
    x_low = lax.rem(x, 2)
    rest = w_in.shape[0] - LANES
    for there in range(SIDE):
        at = there * pair
        low = embeds[LANES:, at : at + pair]
        low = jnp.concatenate([low[:, :rows], low[:, rows:]], axis=0)
        low = jnp.concatenate([low, jnp.zeros((2 * rest, 2 * LANES - rows), BF16)], axis=1)
        top = embeds[0:LANES, at : at + pair].T
        for which in range(2):
            start = pl.multiple_of(jnp.where(x_low == which, pair, 0), 16)
            embed_out[there, pl.ds(start, rows)] = top[which * rows : (which + 1) * rows]
        embed_out[there, rows:pair] = low.T[:rows]
    e_z = {}
    for late, area in enumerate((slice(0, pair), slice(pair, pair + rows))):
        for d in (1, 3, 2):
            e_z[late, d] = send(
                embed_out.at[lax.rem(z + d, SIDE), area], embed_all.at[d - 1, area],
                e_send.at[late, d - 1], e_recv.at[late, d - 1], z_to[d],
            )
    for d in (1, 3, 2):
        w_z[d].wait_recv()
        w_c[d] = send(
            w_all.at[d, core], w_all.at[d, core], w_send.at[d + 2], w_recv.at[d + 2], sibling
        )
    lane = lax.broadcasted_iota(jnp.int32, (rows, LANES), 1)

    def part_sum(late, side):
        which = x_low if late else 1 - x_low
        summed = None
        for d in (0, 1, 3, 2):
            features = embed_out.at[z] if d == 0 else embed_all.at[d - 1]
            first = features[pair : pair + rows, :] if late else features[0:rows, :]
            second = features[rows:pair, :]
            second = jnp.where(lane // rest == which, second, jnp.zeros((), BF16))
            weight = w_all[d, side]
            weight = jnp.concatenate([weight, weight[LANES:]], axis=0)
            term = jnp.dot(
                jnp.concatenate([first, second], axis=1), weight, preferred_element_type=F32
            )
            summed = term if summed is None else summed + term
        return summed

    for d in (1, 3, 2):
        w_c[d].wait_recv()
    for d in (1, 3, 2):
        e_z[0, d].wait_recv()
    given = []
    partner = device(x + 1 - 2 * x_low, y, z, core)
    for side in range(2):
        partial[side] = part_sum(False, side).astype(BF16)
        given.append(send(
            partial.at[side], arrived.at[side], part_send.at[side], part_recv.at[side], partner
        ))
    for d in (1, 3, 2):
        e_z[1, d].wait_recv()
    own = [part_sum(True, side) for side in range(2)]
    for side in range(2):
        given[side].wait_recv()
        own[side] = own[side] + arrived[side].astype(F32)
    hidden = jnp.concatenate(own, axis=1).astype(BF16).astype(F32)
    normed = norm_rows(hidden, gain_attn[...][None, :])

    loads[3].wait()
    kv_y = {}
    q_y = {}

    def exchange_kv(head):
        for part in range(SIDE):
            at = part * SHARE + head * SIZE
            kv_out[head, part] = jnp.concatenate(
                [keys[:, at : at + SIZE], values[:, at : at + SIZE]], axis=1
            ).astype(BF16)
        for d in ahead:
            kv_y[head, d] = send(
                kv_out.at[head, lax.rem(y + d, SIDE)], kv_all.at[head, 0, pl.ds(d * rows, rows)],
                y_send.at[head, d - 1], y_recv.at[head, d - 1], y_to[d],
            )
        kv_all[head, 0, 0:rows] = kv_out[head, y]

    def exchange_q(head):
        for part in range(SIDE):
            at = part * SHARE + head * SIZE
            piece = query[:, at : at + SIZE] * (
                temper[part * TEAM + head] * (SIZE ** (-0.5) * LOG2E)
            )
            q_out[head, part] = fold(piece)
        for d in ahead:
            q_y[head, d] = send(
                q_out.at[head, lax.rem(y + d, SIDE)], q_all.at[head, 0, pl.ds(d * FOLD, FOLD)],
                y_send.at[TEAM + head, d - 1], y_recv.at[TEAM + head, d - 1], y_to[d],
            )
        q_all[head, 0, 0:FOLD] = q_out[head, y]

    query = jnp.dot(normed, w_qkv[:, :width], preferred_element_type=F32)
    exchange_q(0)
    keys = jnp.dot(normed, w_qkv[:, width : 2 * width], preferred_element_type=F32)
    values = jnp.dot(normed, w_qkv[:, 2 * width :], preferred_element_type=F32)
    exchange_kv(0)
    exchange_kv(1)
    exchange_q(1)
    exchange_kv(2)
    exchange_q(2)

    kv_z = {}
    kv_c = {}
    q_x = {}

    def spread_kv(head):
        for d in ahead:
            kv_y[head, d].wait_recv()
        own = kv_all.at[head, 0]
        for d in (1, 3, 2):
            kv_z[head, Z_SLOT[d]] = send(
                own, kv_all.at[head, Z_SLOT[d]], z_send.at[head, d - 1],
                kv_recv.at[head, Z_SLOT[d]], z_to[d],
            )
        forward_kv(head, 0)

    def forward_kv(head, slot):
        to = FORWARD[slot]
        kv_c[head, to] = remote(
            kv_all.at[head, slot], kv_all.at[head, to], c_send.at[head, to],
            kv_recv.at[head, to], sibling,
        )
        kv_c[head, to].start()

    def spread_q(head):
        for d in ahead:
            q_y[head, d].wait_recv()
        for d in (1, 3, 2):
            q_x[head, d] = send(
                q_all.at[head, 0], q_all.at[head, d], x_send.at[head, d - 1],
                x_recv.at[head, d - 1], x_to[d],
            )

    spread_q(0)
    spread_kv(0)
    spread_kv(1)
    spread_q(1)
    spread_kv(2)
    spread_q(2)

    columns = turned.shape[1]
    ones = jnp.ones((8, block), BF16)
    o_x, l_x = {}, {}
    for head in range(TEAM):
        for d in ahead:
            q_x[head, d].wait_recv()
        for slot in range(SIDE):
            part = unfold(q_all.at[head, slot], rows)
            part = jnp.concatenate([part, jnp.zeros((block, LANES - SIZE), BF16)], axis=1)
            turned[:, slot * block : (slot + 1) * block] = part.T
        acc[...] = jnp.zeros(acc.shape, F32)
        peak[...] = jnp.full(peak.shape, -1e30, F32)

        strips = [slice(at, at + STRIP) for at in range(0, columns, STRIP)]

        def score(slot, into, strip, head=head):
            into[:, strip] = jnp.dot(
                kv_all[head, slot], turned[:, strip], preferred_element_type=F32
            )

        def absorb(values, scores_ref, strip):
            scores = scores_ref[:, strip]
            before = peak[0:1, strip]
            after = jnp.maximum(before, jnp.max(scores, axis=0, keepdims=True))
            peak[0:1, strip] = after
            weights = jnp.exp2(scores - after).astype(BF16)
            acc[:, strip] = acc[:, strip] * jnp.exp2(before - after) + jnp.dot(
                values, weights, preferred_element_type=F32
            )

        def step_over(slot, now, later, into, head=head):
            values = jnp.concatenate([kv_all[head, slot].T[SIZE:], ones], axis=0)
            for strip in strips:
                score(later, into, strip)
                absorb(values, now, strip)

        def wait_slot(slot, head=head):
            pltpu.make_async_copy(
                kv_all.at[head, slot], kv_all.at[head, slot], kv_recv.at[head, slot]
            ).wait()

        for strip in strips:
            score(0, score_a, strip)

        def pair(step, _, head=head):
            @pl.when(step == 0)
            def _():
                wait_slot(2)
                forward_kv(head, 2)
                wait_slot(1)

            @pl.when(step == 1)
            def _():
                wait_slot(3)
                forward_kv(head, 3)
                wait_slot(4)

            @pl.when(step == 2)
            def _():
                wait_slot(6)
                forward_kv(head, 6)
                wait_slot(5)

            @pl.when(step == 3)
            def _():
                wait_slot(7)

            step_over(2 * step, score_a, 2 * step + 1, score_b)
            step_over(2 * step + 1, score_b, jnp.minimum(2 * step + 2, SLOTS - 1), score_a)
            return 0

        lax.fori_loop(0, SLOTS // 2, pair, 0)

        sums_row = acc[SIZE : SIZE + 1, :]
        log_sum = peak[0:1, :] + jnp.log2(sums_row)
        whole = jnp.concatenate(
            [acc[0:SIZE, :] * (1.0 / sums_row), jnp.zeros((LANES - SIZE, columns), F32)], axis=0
        )
        for slot in (1, 3, 2, 0):
            area = slice(slot * block, (slot + 1) * block)
            upright = whole[:, area].T[:, :SIZE]
            for d in range(SIDE):
                o_out[head, slot, d * FOLD : (d + 1) * FOLD] = fold(
                    upright[d * rows : (d + 1) * rows]
                )
            spare = l_out.shape[3] - block
            line = jnp.concatenate([log_sum[:, area], jnp.zeros((1, spare), F32)], axis=1)
            l_out[head, slot] = jnp.broadcast_to(line, l_out.shape[2:])
            if slot:
                to = x_to[SIDE - slot]
                o_x[head, slot] = send(
                    o_out.at[head, slot], o_in.at[head, slot - 1], o_send.at[head, slot - 1],
                    o_recv.at[head, slot - 1], to,
                )
                l_x[head, slot] = send(
                    l_out.at[head, slot], l_in.at[head, slot - 1], o_send.at[head, slot + 2],
                    o_recv.at[head, slot + 2], to,
                )

    def merge(head):
        for slot in ahead:
            o_x[head, slot].wait_recv()
            l_x[head, slot].wait_recv()
        logs = [l_out[head, 0, 0:1]] + [l_in[head, slot - 1, 0:1] for slot in ahead]
        top = functools.reduce(jnp.maximum, logs)
        shares = [jnp.exp2(log - top) for log in logs]
        inverse = 1.0 / functools.reduce(jnp.add, shares)
        shares = [share * inverse for share in shares]
        shares = jnp.concatenate(shares + shares, axis=0).T
        pieces = [o_out.at[head, 0]] + [o_in.at[head, slot - 1] for slot in ahead]
        return functools.reduce(
            jnp.add,
            [
                unfold(piece, rows).astype(F32) * shares[:block, i : i + 1]
                for i, piece in enumerate(pieces)
            ],
        )

    b_y = {}

    def give_back(tile, value):
        mine[tile] = value.astype(BF16)
        for d in ahead:
            b_y[tile, d] = send(
                mine.at[tile, pl.ds(d * rows, rows)], back.at[tile, d],
                b_send.at[tile, d - 1], b_recv.at[tile, d - 1], y_to[SIDE - d],
            )

    give_back(0, jnp.concatenate([merge(0), merge(1)], axis=1))
    give_back(1, jnp.concatenate([merge(2), jnp.zeros((block, SIZE), F32)], axis=1))
    mixed = hidden
    loads[4].wait()
    for tile in range(2):
        used = LANES if tile == 0 else SIZE
        for d in range(SIDE):
            if d:
                b_y[tile, d].wait_recv()
                piece = back[tile, d]
            else:
                piece = mine[tile, 0:rows]
            owner = lax.rem(y + d, SIDE)
            start = pl.multiple_of(owner * SHARE + tile * LANES, 16)
            mixed = mixed + jnp.dot(
                piece[:, :used], w_out[pl.ds(start, used), :], preferred_element_type=F32
            )
    resid = mixed.astype(BF16).astype(F32)
    normed = norm_rows(resid, gain_mlp[...][None, :])
    loads[5].wait()
    loads[6].wait()
    encoded = resid
    for at in range(0, w_up.shape[1], width):
        raised = jnp.dot(normed, w_up[:, at : at + width], preferred_element_type=F32)
        active = jax.nn.gelu(raised).astype(BF16)
        encoded = encoded + jnp.dot(active, w_down[at : at + width, :], preferred_element_type=F32)
    out_ref[...] = encoded.astype(BF16)
    for copy in copies:
        copy.wait_send()
    for head in range(TEAM):
        for slot, to in FORWARD.items():
            pltpu.make_async_copy(
                kv_all.at[head, slot], kv_all.at[head, slot], c_send.at[head, to]
            ).wait()


def on_device(tile_embeds, w_in, perturb, gain_attn, w_qkv, temper, w_out, gain_mlp, w_up, w_down):
    width = w_qkv.shape[0]
    rows = tile_embeds.shape[1] // GROUPS
    block = SIDE * rows
    columns = SIDE * block
    dma = pltpu.SemaphoreType.DMA
    vmem = pltpu.VMEM
    return pl.pallas_call(
        layer_kernel,
        out_shape=jax.ShapeDtypeStruct((rows, width), BF16),
        in_specs=[ANY, ANY, ANY, VMEM, ANY, SMEM, ANY, VMEM, ANY, ANY],
        out_specs=VMEM,
        scratch_shapes=[
            vmem(tile_embeds.shape, BF16), vmem(w_in.shape, BF16), vmem(perturb.shape, BF16),
            vmem(w_qkv.shape, BF16), vmem(w_out.shape, BF16), vmem(w_up.shape, BF16),
            vmem(w_down.shape, BF16),
            vmem((SIDE, 2, w_in.shape[0], width // 2), BF16),
            vmem((SIDE, 3 * rows, LANES), BF16),
            vmem((SIDE - 1, 3 * rows, LANES), BF16),
            vmem((2, rows, width // 2), BF16),
            vmem((2, rows, width // 2), BF16),
            vmem((TEAM, SIDE, FOLD, LANES), BF16),
            vmem((TEAM, SIDE, rows, LANES), BF16),
            vmem((TEAM, SIDE, SIDE * FOLD, LANES), BF16),
            vmem((TEAM, SLOTS, block, LANES), BF16),
            vmem((LANES, columns), BF16),
            vmem((block, columns), F32),
            vmem((block, columns), F32),
            vmem((SIZE + 8, columns), F32),
            vmem((8, columns), F32),
            vmem((TEAM, SIDE, SIDE * FOLD, LANES), BF16),
            vmem((TEAM, SIDE - 1, SIDE * FOLD, LANES), BF16),
            vmem((TEAM, SIDE, 8, 640), F32),
            vmem((TEAM, SIDE - 1, 8, 640), F32),
            vmem((2, block, LANES), BF16),
            vmem((2, SIDE, rows, LANES), BF16),
            dma((7,)), dma((6,)), dma((6,)), dma((2, 3)), dma((2, 3)), dma((2,)), dma((2,)),
            dma((6, 3)), dma((6, 3)), dma((TEAM, 3)), dma((TEAM, 3)),
            dma((TEAM, 3)), dma((TEAM, SLOTS)), dma((TEAM, SLOTS)),
            dma((TEAM, 6)), dma((TEAM, 6)), dma((2, 3)), dma((2, 3)),
        ],
        compiler_params=pltpu.CompilerParams(
            collective_id=0, has_side_effects=True, vmem_limit_bytes=56 * 2**20
        ),
        name="layer",
    )(tile_embeds, w_in, perturb, gain_attn, w_qkv, temper, w_out, gain_mlp, w_up, w_down)


def solution(mesh):
    placed = (P("grp", "seq"), P("grp", None), P("grp", None), P(), P(), P(), P(), P(), P(), P())
    return jax.shard_map(
        on_device, mesh=mesh, in_specs=placed, out_specs=P(("seq", "grp"), None), check_vma=False
    )
```

```python
import functools

import jax
import jax.numpy as jnp
from jax import lax
from jax.experimental import pallas as pl
from jax.experimental.pallas import tpu as pltpu
from jax.sharding import PartitionSpec as P

MESH = pl.DeviceIdType.MESH
ANY = pl.BlockSpec(memory_space=pl.ANY)
VMEM = pl.BlockSpec(memory_space=pltpu.VMEM)
SMEM = pl.BlockSpec(memory_space=pltpu.SMEM)
BF16 = jnp.bfloat16
F32 = jnp.float32
LOG2E = 1.4426950408889634
SIDE = 4
GROUPS = 8
TEAM = 3
SIZE = 64
SHARE = TEAM * SIZE
LANES = 128
SLOTS = 8
FOLD = 80
STRIP = 256
FORWARD = {0: 1, 2: 4, 3: 5, 6: 7}
Z_SLOT = {1: 2, 3: 3, 2: 6}


def position():
    seq, grp = lax.axis_index("seq"), lax.axis_index("grp")
    x = (seq // 8) * 2 + grp % 2
    return x, (seq // 2) % 4, grp // 2, seq % 2


def device(x, y, z, core):
    return ((x // 2) * 8 + y * 2 + core, z * 2 + x % 2)


def remote(src, dst, send_sem, recv_sem, partner):
    return pltpu.make_async_remote_copy(
        src_ref=src, dst_ref=dst, send_sem=send_sem, recv_sem=recv_sem,
        device_id=partner, device_id_type=MESH,
    )


def fold(piece):
    rows = piece.shape[0]
    blank = jnp.zeros((2 * FOLD - rows, SIZE), piece.dtype)
    lower = jnp.concatenate([piece[FOLD:], blank], axis=0)
    return jnp.concatenate([piece[:FOLD], lower], axis=1).astype(BF16)


def unfold(folded, rows):
    pieces = []
    for at in range(0, folded.shape[0], FOLD):
        pieces += [folded[at : at + FOLD, :SIZE], folded[at : at + rows - FOLD, SIZE:]]
    return jnp.concatenate(pieces, axis=0)


def norm_rows(floats, gain):
    average = jnp.mean(floats, axis=-1, keepdims=True)
    centred = floats - average
    spread = jnp.mean(centred * centred, axis=-1, keepdims=True)
    return (centred * lax.rsqrt(spread + 1e-05) * gain).astype(BF16)


def layer_kernel(
    embeds_hbm, w_in_hbm, perturb_hbm, gain_attn, w_qkv_hbm, temper, w_out_hbm, gain_mlp,
    w_up_hbm, w_down_hbm,
    out_ref,
    embeds, w_in, perturb, w_qkv, w_out, w_up, w_down,
    w_all, embed_out, embed_all, partial, arrived, q_out, kv_out, q_all, kv_all,
    turned, score_a, score_b, acc, peak, o_out, o_in, l_out, l_in, mine, back,
    load_sem, w_send, w_recv, e_send, e_recv, part_send, part_recv, y_send, y_recv, x_send, x_recv, z_send, kv_recv, c_send,
    o_send, o_recv, b_send, b_recv,
):
    x, y, z, core = position()
    rows, width = out_ref.shape
    block = SIDE * rows
    ahead = (1, 2, 3)
    x_to = {d: device(lax.rem(x + d, SIDE), y, z, core) for d in ahead}
    y_to = {d: device(x, lax.rem(y + d, SIDE), z, core) for d in ahead}
    z_to = {d: device(x, y, lax.rem(z + d, SIDE), core) for d in ahead}
    sibling = device(x, y, z, 1 - core)
    loads = [
        pltpu.make_async_copy(src, dst, load_sem.at[i])
        for i, (src, dst) in enumerate([
            (embeds_hbm, embeds), (w_in_hbm, w_in), (perturb_hbm, perturb), (w_qkv_hbm, w_qkv),
            (w_out_hbm, w_out), (w_up_hbm, w_up), (w_down_hbm, w_down),
        ])
    ]
    for load in loads[:3]:
        load.start()
    barrier = pltpu.get_barrier_semaphore()
    greeted = [to[d] for to in (x_to, y_to, z_to) for d in ahead] + [sibling]
    for partner in greeted:
        pl.semaphore_signal(barrier, inc=1, device_id=partner, device_id_type=MESH)
    copies = []

    def send(*args):
        copy = remote(*args)
        copy.start()
        copies.append(copy)
        return copy

    for load in loads[1:3]:
        load.wait()
    half = width // 2
    w_eff = (w_in[...].astype(F32) + perturb[...].astype(F32)).astype(BF16)
    for side in range(2):
        w_all[0, side] = w_eff[:, side * half : (side + 1) * half]
    pl.semaphore_wait(barrier, len(greeted))
    w_z, w_y, w_c = {}, {}, {}
    quarter = w_in.shape[0] // SIDE
    piece = pl.ds(pl.multiple_of(y * quarter, 16), quarter)
    for d in (1, 3, 2):
        w_z[d] = send(
            w_all.at[0, core, piece], w_all.at[d, core, piece],
            w_send.at[0, d - 1], w_recv.at[0, d - 1], z_to[d],
        )
    loads[0].wait()
    pair = 2 * rows
    x_low = lax.rem(x, 2)
    rest = w_in.shape[0] - LANES
    for there in range(SIDE):
        at = there * pair
        low = embeds[LANES:, at : at + pair]
        low = jnp.concatenate([low[:, :rows], low[:, rows:]], axis=0)
        low = jnp.concatenate([low, jnp.zeros((2 * rest, 2 * LANES - rows), BF16)], axis=1)
        top = embeds[0:LANES, at : at + pair].T
        for which in range(2):
            start = pl.multiple_of(jnp.where(x_low == which, pair, 0), 16)
            embed_out[there, pl.ds(start, rows)] = top[which * rows : (which + 1) * rows]
        embed_out[there, rows:pair] = low.T[:rows]
    e_z = {}
    for late, area in enumerate((slice(0, pair), slice(pair, pair + rows))):
        for d in (1, 3, 2):
            e_z[late, d] = send(
                embed_out.at[lax.rem(z + d, SIDE), area], embed_all.at[d - 1, area],
                e_send.at[late, d - 1], e_recv.at[late, d - 1], z_to[d],
            )
    for d in (1, 3, 2):
        w_z[d].wait_recv()
        for e in (1, 3, 2):
            w_y[d, e] = send(
                w_all.at[d, core, piece], w_all.at[d, core, piece],
                w_send.at[e, d - 1], w_recv.at[e, d - 1], y_to[e],
            )
    for d in (1, 3, 2):
        for e in (1, 3, 2):
            w_y[d, e].wait_recv()
        w_c[d] = send(
            w_all.at[d, core], w_all.at[d, core], w_send.at[4, d - 1], w_recv.at[4, d - 1], sibling
        )
    for load in loads[3:]:
        load.start()
    lane = lax.broadcasted_iota(jnp.int32, (rows, LANES), 1)

    def part_sum(late, side):
        which = x_low if late else 1 - x_low
        summed = None
        for d in (0, 1, 3, 2):
            features = embed_out.at[z] if d == 0 else embed_all.at[d - 1]
            first = features[pair : pair + rows, :] if late else features[0:rows, :]
            second = features[rows:pair, :]
            second = jnp.where(lane // rest == which, second, jnp.zeros((), BF16))
            weight = w_all[d, side]
            weight = jnp.concatenate([weight, weight[LANES:]], axis=0)
            term = jnp.dot(
                jnp.concatenate([first, second], axis=1), weight, preferred_element_type=F32
            )
            summed = term if summed is None else summed + term
        return summed

    for d in (1, 3, 2):
        w_c[d].wait_recv()
    for d in (1, 3, 2):
        e_z[0, d].wait_recv()
    given = []
    partner = device(x + 1 - 2 * x_low, y, z, core)
    for side in range(2):
        partial[side] = part_sum(False, side).astype(BF16)
        given.append(send(
            partial.at[side], arrived.at[side], part_send.at[side], part_recv.at[side], partner
        ))
    for d in (1, 3, 2):
        e_z[1, d].wait_recv()
    own = [part_sum(True, side) for side in range(2)]
    for side in range(2):
        given[side].wait_recv()
        own[side] = own[side] + arrived[side].astype(F32)
    hidden = jnp.concatenate(own, axis=1).astype(BF16).astype(F32)
    normed = norm_rows(hidden, gain_attn[...][None, :])

    loads[3].wait()
    kv_y = {}
    q_y = {}

    def exchange_kv(head):
        for part in range(SIDE):
            at = part * SHARE + head * SIZE
            kv_out[head, part] = jnp.concatenate(
                [keys[:, at : at + SIZE], values[:, at : at + SIZE]], axis=1
            ).astype(BF16)
        for d in ahead:
            kv_y[head, d] = send(
                kv_out.at[head, lax.rem(y + d, SIDE)], kv_all.at[head, 0, pl.ds(d * rows, rows)],
                y_send.at[head, d - 1], y_recv.at[head, d - 1], y_to[d],
            )
        kv_all[head, 0, 0:rows] = kv_out[head, y]

    def exchange_q(head):
        for part in range(SIDE):
            at = part * SHARE + head * SIZE
            piece = query[:, at : at + SIZE] * (
                temper[part * TEAM + head] * (SIZE ** (-0.5) * LOG2E)
            )
            q_out[head, part] = fold(piece)
        for d in ahead:
            q_y[head, d] = send(
                q_out.at[head, lax.rem(y + d, SIDE)], q_all.at[head, 0, pl.ds(d * FOLD, FOLD)],
                y_send.at[TEAM + head, d - 1], y_recv.at[TEAM + head, d - 1], y_to[d],
            )
        q_all[head, 0, 0:FOLD] = q_out[head, y]

    kv_z = {}
    kv_c = {}
    q_x = {}

    def spread_kv(head):
        for d in ahead:
            kv_y[head, d].wait_recv()
        own = kv_all.at[head, 0]
        for d in (1, 3, 2):
            kv_z[head, Z_SLOT[d]] = send(
                own, kv_all.at[head, Z_SLOT[d]], z_send.at[head, d - 1],
                kv_recv.at[head, Z_SLOT[d]], z_to[d],
            )
        forward_kv(head, 0)

    def forward_kv(head, slot):
        to = FORWARD[slot]
        kv_c[head, to] = remote(
            kv_all.at[head, slot], kv_all.at[head, to], c_send.at[head, to],
            kv_recv.at[head, to], sibling,
        )
        kv_c[head, to].start()

    def spread_q(head):
        for d in ahead:
            q_y[head, d].wait_recv()
        for d in (1, 3, 2):
            q_x[head, d] = send(
                q_all.at[head, 0], q_all.at[head, d], x_send.at[head, d - 1],
                x_recv.at[head, d - 1], x_to[d],
            )

    query = jnp.dot(normed, w_qkv[:, :width], preferred_element_type=F32)
    exchange_q(0)
    keys = jnp.dot(normed, w_qkv[:, width : 2 * width], preferred_element_type=F32)
    values = jnp.dot(normed, w_qkv[:, 2 * width :], preferred_element_type=F32)
    exchange_kv(0)
    spread_q(0)
    exchange_kv(1)
    exchange_q(1)
    spread_kv(0)
    exchange_kv(2)
    exchange_q(2)
    spread_kv(1)
    spread_q(1)
    spread_kv(2)
    spread_q(2)

    columns = turned.shape[1]
    ones = jnp.ones((8, block), BF16)
    o_x, l_x = {}, {}
    for head in range(TEAM):
        for d in ahead:
            q_x[head, d].wait_recv()
        for slot in range(SIDE):
            part = unfold(q_all.at[head, slot], rows)
            part = jnp.concatenate([part, jnp.zeros((block, LANES - SIZE), BF16)], axis=1)
            turned[:, slot * block : (slot + 1) * block] = part.T
        acc[...] = jnp.zeros(acc.shape, F32)
        peak[...] = jnp.full(peak.shape, -1e30, F32)

        strips = [slice(at, at + STRIP) for at in range(0, columns, STRIP)]

        def score(slot, into, strip, head=head):
            into[:, strip] = jnp.dot(
                kv_all[head, slot], turned[:, strip], preferred_element_type=F32
            )

        def absorb(values, scores_ref, strip):
            scores = scores_ref[:, strip]
            before = peak[0:1, strip]
            after = jnp.maximum(before, jnp.max(scores, axis=0, keepdims=True))
            peak[0:1, strip] = after
            weights = jnp.exp2(scores - after).astype(BF16)
            acc[:, strip] = acc[:, strip] * jnp.exp2(before - after) + jnp.dot(
                values, weights, preferred_element_type=F32
            )

        def step_over(slot, now, later, into, head=head):
            values = jnp.concatenate([kv_all[head, slot].T[SIZE:], ones], axis=0)
            for strip in strips:
                score(later, into, strip)
                absorb(values, now, strip)

        def wait_slot(slot, head=head):
            pltpu.make_async_copy(
                kv_all.at[head, slot], kv_all.at[head, slot], kv_recv.at[head, slot]
            ).wait()

        for strip in strips:
            score(0, score_a, strip)

        def pair(step, _, head=head):
            @pl.when(step == 0)
            def _():
                wait_slot(2)
                forward_kv(head, 2)
                wait_slot(1)

            @pl.when(step == 1)
            def _():
                wait_slot(3)
                forward_kv(head, 3)
                wait_slot(4)

            @pl.when(step == 2)
            def _():
                wait_slot(6)
                forward_kv(head, 6)
                wait_slot(5)

            @pl.when(step == 3)
            def _():
                wait_slot(7)

            step_over(2 * step, score_a, 2 * step + 1, score_b)
            step_over(2 * step + 1, score_b, jnp.minimum(2 * step + 2, SLOTS - 1), score_a)
            return 0

        lax.fori_loop(0, SLOTS // 2, pair, 0)

        sums_row = acc[SIZE : SIZE + 1, :]
        log_sum = peak[0:1, :] + jnp.log2(sums_row)
        whole = jnp.concatenate(
            [acc[0:SIZE, :] * (1.0 / sums_row), jnp.zeros((LANES - SIZE, columns), F32)], axis=0
        )
        for slot in (1, 3, 2, 0):
            area = slice(slot * block, (slot + 1) * block)
            upright = whole[:, area].T[:, :SIZE]
            for d in range(SIDE):
                o_out[head, slot, d * FOLD : (d + 1) * FOLD] = fold(
                    upright[d * rows : (d + 1) * rows]
                )
            spare = l_out.shape[3] - block
            line = jnp.concatenate([log_sum[:, area], jnp.zeros((1, spare), F32)], axis=1)
            l_out[head, slot] = jnp.broadcast_to(line, l_out.shape[2:])
            if slot:
                to = x_to[SIDE - slot]
                o_x[head, slot] = send(
                    o_out.at[head, slot], o_in.at[head, slot - 1], o_send.at[head, slot - 1],
                    o_recv.at[head, slot - 1], to,
                )
                l_x[head, slot] = send(
                    l_out.at[head, slot], l_in.at[head, slot - 1], o_send.at[head, slot + 2],
                    o_recv.at[head, slot + 2], to,
                )

    def merge(head):
        for slot in ahead:
            o_x[head, slot].wait_recv()
            l_x[head, slot].wait_recv()
        logs = [l_out[head, 0, 0:1]] + [l_in[head, slot - 1, 0:1] for slot in ahead]
        top = functools.reduce(jnp.maximum, logs)
        shares = [jnp.exp2(log - top) for log in logs]
        inverse = 1.0 / functools.reduce(jnp.add, shares)
        shares = [share * inverse for share in shares]
        shares = jnp.concatenate(shares + shares, axis=0).T
        pieces = [o_out.at[head, 0]] + [o_in.at[head, slot - 1] for slot in ahead]
        return functools.reduce(
            jnp.add,
            [
                unfold(piece, rows).astype(F32) * shares[:block, i : i + 1]
                for i, piece in enumerate(pieces)
            ],
        )

    b_y = {}

    def give_back(tile, value):
        mine[tile] = value.astype(BF16)
        for d in ahead:
            b_y[tile, d] = send(
                mine.at[tile, pl.ds(d * rows, rows)], back.at[tile, d],
                b_send.at[tile, d - 1], b_recv.at[tile, d - 1], y_to[SIDE - d],
            )

    give_back(0, jnp.concatenate([merge(0), merge(1)], axis=1))
    give_back(1, jnp.concatenate([merge(2), jnp.zeros((block, SIZE), F32)], axis=1))
    mixed = hidden
    loads[4].wait()
    for tile in range(2):
        used = LANES if tile == 0 else SIZE
        for d in range(SIDE):
            if d:
                b_y[tile, d].wait_recv()
                piece = back[tile, d]
            else:
                piece = mine[tile, 0:rows]
            owner = lax.rem(y + d, SIDE)
            start = pl.multiple_of(owner * SHARE + tile * LANES, 16)
            mixed = mixed + jnp.dot(
                piece[:, :used], w_out[pl.ds(start, used), :], preferred_element_type=F32
            )
    resid = mixed.astype(BF16).astype(F32)
    normed = norm_rows(resid, gain_mlp[...][None, :])
    loads[5].wait()
    loads[6].wait()
    encoded = resid
    for at in range(0, w_up.shape[1], width):
        raised = jnp.dot(normed, w_up[:, at : at + width], preferred_element_type=F32)
        active = jax.nn.gelu(raised).astype(BF16)
        encoded = encoded + jnp.dot(active, w_down[at : at + width, :], preferred_element_type=F32)
    out_ref[...] = encoded.astype(BF16)
    for copy in copies:
        copy.wait_send()
    for head in range(TEAM):
        for slot, to in FORWARD.items():
            pltpu.make_async_copy(
                kv_all.at[head, slot], kv_all.at[head, slot], c_send.at[head, to]
            ).wait()


def on_device(tile_embeds, w_in, perturb, gain_attn, w_qkv, temper, w_out, gain_mlp, w_up, w_down):
    width = w_qkv.shape[0]
    rows = tile_embeds.shape[1] // GROUPS
    block = SIDE * rows
    columns = SIDE * block
    dma = pltpu.SemaphoreType.DMA
    vmem = pltpu.VMEM
    return pl.pallas_call(
        layer_kernel,
        out_shape=jax.ShapeDtypeStruct((rows, width), BF16),
        in_specs=[ANY, ANY, ANY, VMEM, ANY, SMEM, ANY, VMEM, ANY, ANY],
        out_specs=VMEM,
        scratch_shapes=[
            vmem(tile_embeds.shape, BF16), vmem(w_in.shape, BF16), vmem(perturb.shape, BF16),
            vmem(w_qkv.shape, BF16), vmem(w_out.shape, BF16), vmem(w_up.shape, BF16),
            vmem(w_down.shape, BF16),
            vmem((SIDE, 2, w_in.shape[0], width // 2), BF16),
            vmem((SIDE, 3 * rows, LANES), BF16),
            vmem((SIDE - 1, 3 * rows, LANES), BF16),
            vmem((2, rows, width // 2), BF16),
            vmem((2, rows, width // 2), BF16),
            vmem((TEAM, SIDE, FOLD, LANES), BF16),
            vmem((TEAM, SIDE, rows, LANES), BF16),
            vmem((TEAM, SIDE, SIDE * FOLD, LANES), BF16),
            vmem((TEAM, SLOTS, block, LANES), BF16),
            vmem((LANES, columns), BF16),
            vmem((block, columns), F32),
            vmem((block, columns), F32),
            vmem((SIZE + 8, columns), F32),
            vmem((8, columns), F32),
            vmem((TEAM, SIDE, SIDE * FOLD, LANES), BF16),
            vmem((TEAM, SIDE - 1, SIDE * FOLD, LANES), BF16),
            vmem((TEAM, SIDE, 8, 640), F32),
            vmem((TEAM, SIDE - 1, 8, 640), F32),
            vmem((2, block, LANES), BF16),
            vmem((2, SIDE, rows, LANES), BF16),
            dma((7,)), dma((5, 3)), dma((5, 3)), dma((2, 3)), dma((2, 3)), dma((2,)), dma((2,)),
            dma((6, 3)), dma((6, 3)), dma((TEAM, 3)), dma((TEAM, 3)),
            dma((TEAM, 3)), dma((TEAM, SLOTS)), dma((TEAM, SLOTS)),
            dma((TEAM, 6)), dma((TEAM, 6)), dma((2, 3)), dma((2, 3)),
        ],
        compiler_params=pltpu.CompilerParams(
            collective_id=0, has_side_effects=True, vmem_limit_bytes=56 * 2**20
        ),
        name="layer",
    )(tile_embeds, w_in, perturb, gain_attn, w_qkv, temper, w_out, gain_mlp, w_up, w_down)


def solution(mesh):
    placed = (P("grp", "seq"), P("grp", None), P("grp", None), P(), P(), P(), P(), P(), P(), P())
    return jax.shard_map(
        on_device, mesh=mesh, in_specs=placed, out_specs=P(("seq", "grp"), None), check_vma=False
    )
```

```python
import functools

import jax
import jax.numpy as jnp
from jax import lax
from jax.experimental import pallas as pl
from jax.experimental.pallas import tpu as pltpu
from jax.sharding import PartitionSpec as P

MESH = pl.DeviceIdType.MESH
ANY = pl.BlockSpec(memory_space=pl.ANY)
VMEM = pl.BlockSpec(memory_space=pltpu.VMEM)
SMEM = pl.BlockSpec(memory_space=pltpu.SMEM)
BF16 = jnp.bfloat16
F32 = jnp.float32
LOG2E = 1.4426950408889634
SIDE = 4
GROUPS = 8
TEAM = 3
SIZE = 64
SHARE = TEAM * SIZE
LANES = 128
SLOTS = 8
FOLD = 80
STRIP = 256
FORWARD = {0: 1, 2: 4, 3: 5, 6: 7}
Z_SLOT = {1: 2, 3: 3, 2: 6}


def position():
    seq, grp = lax.axis_index("seq"), lax.axis_index("grp")
    x = (seq // 8) * 2 + grp % 2
    return x, (seq // 2) % 4, grp // 2, seq % 2


def device(x, y, z, core):
    return ((x // 2) * 8 + y * 2 + core, z * 2 + x % 2)


def remote(src, dst, send_sem, recv_sem, partner):
    return pltpu.make_async_remote_copy(
        src_ref=src, dst_ref=dst, send_sem=send_sem, recv_sem=recv_sem,
        device_id=partner, device_id_type=MESH,
    )


def fold(piece):
    rows = piece.shape[0]
    blank = jnp.zeros((2 * FOLD - rows, SIZE), piece.dtype)
    lower = jnp.concatenate([piece[FOLD:], blank], axis=0)
    return jnp.concatenate([piece[:FOLD], lower], axis=1).astype(BF16)


def unfold(folded, rows):
    pieces = []
    for at in range(0, folded.shape[0], FOLD):
        pieces += [folded[at : at + FOLD, :SIZE], folded[at : at + rows - FOLD, SIZE:]]
    return jnp.concatenate(pieces, axis=0)


def norm_rows(floats, gain):
    average = jnp.mean(floats, axis=-1, keepdims=True)
    centred = floats - average
    spread = jnp.mean(centred * centred, axis=-1, keepdims=True)
    return (centred * lax.rsqrt(spread + 1e-05) * gain).astype(BF16)


def layer_kernel(
    embeds_hbm, w_in_hbm, perturb_hbm, gain_attn, w_qkv_hbm, temper, w_out_hbm, gain_mlp,
    w_up_hbm, w_down_hbm,
    out_ref,
    embeds, w_in, perturb, w_qkv, w_out, w_up, w_down,
    w_all, embed_out, embed_all, partial, arrived, q_out, kv_out, q_all, kv_all,
    turned, score_a, score_b, acc, peak, o_out, o_in, l_out, l_in, mine, back,
    load_sem, w_send, w_recv, e_send, e_recv, part_send, part_recv, y_send, y_recv, x_send, x_recv, z_send, kv_recv, c_send,
    o_send, o_recv, b_send, b_recv,
):
    x, y, z, core = position()
    rows, width = out_ref.shape
    block = SIDE * rows
    ahead = (1, 2, 3)
    x_to = {d: device(lax.rem(x + d, SIDE), y, z, core) for d in ahead}
    y_to = {d: device(x, lax.rem(y + d, SIDE), z, core) for d in ahead}
    z_to = {d: device(x, y, lax.rem(z + d, SIDE), core) for d in ahead}
    sibling = device(x, y, z, 1 - core)
    loads = [
        pltpu.make_async_copy(src, dst, load_sem.at[i])
        for i, (src, dst) in enumerate([
            (embeds_hbm, embeds), (w_in_hbm, w_in), (perturb_hbm, perturb), (w_qkv_hbm, w_qkv),
            (w_out_hbm, w_out), (w_up_hbm, w_up), (w_down_hbm, w_down),
        ])
    ]
    for load in loads[:3]:
        load.start()
    barrier = pltpu.get_barrier_semaphore()
    greeted = [to[d] for to in (x_to, y_to, z_to) for d in ahead] + [sibling]
    for partner in greeted:
        pl.semaphore_signal(barrier, inc=1, device_id=partner, device_id_type=MESH)
    copies = []

    def send(*args):
        copy = remote(*args)
        copy.start()
        copies.append(copy)
        return copy

    for load in loads[1:3]:
        load.wait()
    half = width // 2
    w_eff = (w_in[...].astype(F32) + perturb[...].astype(F32)).astype(BF16)
    for side in range(2):
        w_all[0, side] = w_eff[:, side * half : (side + 1) * half]
    pl.semaphore_wait(barrier, len(greeted))
    w_z, w_y, w_c = {}, {}, {}
    quarter = w_in.shape[0] // SIDE
    piece = pl.ds(pl.multiple_of(y * quarter, 16), quarter)
    for d in (1, 3, 2):
        w_z[d] = send(
            w_all.at[0, core, piece], w_all.at[d, core, piece],
            w_send.at[0, d - 1], w_recv.at[0, d - 1], z_to[d],
        )
    loads[0].wait()
    pair = 2 * rows
    x_low = lax.rem(x, 2)
    rest = w_in.shape[0] - LANES
    for there in range(SIDE):
        at = there * pair
        low = embeds[LANES:, at : at + pair]
        low = jnp.concatenate([low[:, :rows], low[:, rows:]], axis=0)
        low = jnp.concatenate([low, jnp.zeros((2 * rest, 2 * LANES - rows), BF16)], axis=1)
        top = embeds[0:LANES, at : at + pair].T
        for which in range(2):
            start = pl.multiple_of(jnp.where(x_low == which, pair, 0), 16)
            embed_out[there, pl.ds(start, rows)] = top[which * rows : (which + 1) * rows]
        embed_out[there, rows:pair] = low.T[:rows]
    e_z = {}
    for late, area in enumerate((slice(0, pair), slice(pair, pair + rows))):
        for d in (1, 3, 2):
            e_z[late, d] = send(
                embed_out.at[lax.rem(z + d, SIDE), area], embed_all.at[d - 1, area],
                e_send.at[late, d - 1], e_recv.at[late, d - 1], z_to[d],
            )
    for d in (1, 3, 2):
        w_z[d].wait_recv()
        for e in (1, 3, 2):
            w_y[d, e] = send(
                w_all.at[d, core, piece], w_all.at[d, core, piece],
                w_send.at[e, d - 1], w_recv.at[e, d - 1], y_to[e],
            )
    for d in (1, 3, 2):
        for e in (1, 3, 2):
            w_y[d, e].wait_recv()
        w_c[d] = send(
            w_all.at[d, core], w_all.at[d, core], w_send.at[4, d - 1], w_recv.at[4, d - 1], sibling
        )
    for load in loads[3:]:
        load.start()
    lane = lax.broadcasted_iota(jnp.int32, (rows, LANES), 1)

    def part_sum(late, side):
        which = x_low if late else 1 - x_low
        summed = None
        for d in (0, 1, 3, 2):
            features = embed_out.at[z] if d == 0 else embed_all.at[d - 1]
            first = features[pair : pair + rows, :] if late else features[0:rows, :]
            second = features[rows:pair, :]
            second = jnp.where(lane // rest == which, second, jnp.zeros((), BF16))
            weight = w_all[d, side]
            weight = jnp.concatenate([weight, weight[LANES:]], axis=0)
            term = jnp.dot(
                jnp.concatenate([first, second], axis=1), weight, preferred_element_type=F32
            )
            summed = term if summed is None else summed + term
        return summed

    for d in (1, 3, 2):
        w_c[d].wait_recv()
    for d in (1, 3, 2):
        e_z[0, d].wait_recv()
    given = []
    partner = device(x + 1 - 2 * x_low, y, z, core)
    for side in range(2):
        partial[side] = part_sum(False, side).astype(BF16)
        given.append(send(
            partial.at[side], arrived.at[side], part_send.at[side], part_recv.at[side], partner
        ))
    for d in (1, 3, 2):
        e_z[1, d].wait_recv()
    own = [part_sum(True, side) for side in range(2)]
    for side in range(2):
        given[side].wait_recv()
        own[side] = own[side] + arrived[side].astype(F32)
    hidden = jnp.concatenate(own, axis=1).astype(BF16).astype(F32)
    normed = norm_rows(hidden, gain_attn[...][None, :])

    loads[3].wait()
    kv_y = {}
    q_y = {}

    def exchange_kv(head):
        for part in range(SIDE):
            at = part * SHARE + head * SIZE
            kv_out[head, part] = jnp.concatenate(
                [keys[:, at : at + SIZE], values[:, at : at + SIZE]], axis=1
            ).astype(BF16)
        for d in ahead:
            kv_y[head, d] = send(
                kv_out.at[head, lax.rem(y + d, SIDE)], kv_all.at[head, 0, pl.ds(d * rows, rows)],
                y_send.at[head, d - 1], y_recv.at[head, d - 1], y_to[d],
            )
        kv_all[head, 0, 0:rows] = kv_out[head, y]

    def exchange_q(head):
        for part in range(SIDE):
            at = part * SHARE + head * SIZE
            piece = query[:, at : at + SIZE] * (
                temper[part * TEAM + head] * (SIZE ** (-0.5) * LOG2E)
            )
            q_out[head, part] = fold(piece)
        for d in ahead:
            q_y[head, d] = send(
                q_out.at[head, lax.rem(y + d, SIDE)], q_all.at[head, 0, pl.ds(d * FOLD, FOLD)],
                y_send.at[TEAM + head, d - 1], y_recv.at[TEAM + head, d - 1], y_to[d],
            )
        q_all[head, 0, 0:FOLD] = q_out[head, y]

    kv_z = {}
    kv_c = {}
    q_x = {}

    def spread_kv(head):
        for d in ahead:
            kv_y[head, d].wait_recv()
        own = kv_all.at[head, 0]
        for d in (1, 3, 2):
            kv_z[head, Z_SLOT[d]] = send(
                own, kv_all.at[head, Z_SLOT[d]], z_send.at[head, d - 1],
                kv_recv.at[head, Z_SLOT[d]], z_to[d],
            )
        forward_kv(head, 0)

    def forward_kv(head, slot):
        to = FORWARD[slot]
        kv_c[head, to] = remote(
            kv_all.at[head, slot], kv_all.at[head, to], c_send.at[head, to],
            kv_recv.at[head, to], sibling,
        )
        kv_c[head, to].start()

    def spread_q(head):
        for d in ahead:
            q_y[head, d].wait_recv()
        for d in (1, 3, 2):
            q_x[head, d] = send(
                q_all.at[head, 0], q_all.at[head, d], x_send.at[head, d - 1],
                x_recv.at[head, d - 1], x_to[d],
            )

    query = jnp.dot(normed, w_qkv[:, :width], preferred_element_type=F32)
    exchange_q(0)
    keys = jnp.dot(normed, w_qkv[:, width : 2 * width], preferred_element_type=F32)
    values = jnp.dot(normed, w_qkv[:, 2 * width :], preferred_element_type=F32)
    exchange_kv(0)
    spread_q(0)
    exchange_kv(1)
    exchange_q(1)
    spread_kv(0)
    exchange_kv(2)
    exchange_q(2)
    spread_kv(1)
    spread_q(1)
    spread_kv(2)
    spread_q(2)

    columns = turned.shape[2]
    ones = jnp.ones((8, block), BF16)
    o_x, l_x = {}, {}
    strips = [slice(at, at + STRIP) for at in range(0, columns, STRIP)]

    def await_queries(head):
        for d in ahead:
            q_x[head, d].wait_recv()

    def turn_queries(head):
        for slot in range(SIDE):
            part = unfold(q_all.at[head, slot], rows)
            part = jnp.concatenate([part, jnp.zeros((block, LANES - SIZE), BF16)], axis=1)
            turned[head % 2, :, slot * block : (slot + 1) * block] = part.T

    def score(head, slot, into, strip):
        into[:, strip] = jnp.dot(
            kv_all[head, slot], turned[head % 2, :, strip], preferred_element_type=F32
        )

    await_queries(0)
    turn_queries(0)
    for strip in strips:
        score(0, 0, score_a, strip)
    for head in range(TEAM):
        acc[...] = jnp.zeros(acc.shape, F32)
        peak[...] = jnp.full(peak.shape, -1e30, F32)

        def absorb(values, scores_ref, strip):
            scores = scores_ref[:, strip]
            before = peak[0:1, strip]
            after = jnp.maximum(before, jnp.max(scores, axis=0, keepdims=True))
            peak[0:1, strip] = after
            weights = jnp.exp2(scores - after).astype(BF16)
            acc[:, strip] = acc[:, strip] * jnp.exp2(before - after) + jnp.dot(
                values, weights, preferred_element_type=F32
            )

        def step_over(slot, now, later, into, head=head):
            values = jnp.concatenate([kv_all[head, slot].T[SIZE:], ones], axis=0)
            for strip in strips:
                if later is not None:
                    score(*later, into, strip)
                absorb(values, now, strip)

        def wait_slot(slot, head=head):
            pltpu.make_async_copy(
                kv_all.at[head, slot], kv_all.at[head, slot], kv_recv.at[head, slot]
            ).wait()

        def pair(step, _, head=head):
            @pl.when(step == 0)
            def _():
                wait_slot(2)
                forward_kv(head, 2)
                wait_slot(1)

            @pl.when(step == 1)
            def _():
                wait_slot(3)
                forward_kv(head, 3)
                wait_slot(4)

            @pl.when(step == 2)
            def _():
                wait_slot(6)
                forward_kv(head, 6)
                wait_slot(5)

            step_over(2 * step, score_a, (head, 2 * step + 1), score_b)
            step_over(2 * step + 1, score_b, (head, 2 * step + 2), score_a)
            return 0

        lax.fori_loop(0, SLOTS // 2 - 1, pair, 0)
        wait_slot(SLOTS - 1)
        follows = head + 1 < TEAM
        if follows:
            await_queries(head + 1)
        step_over(SLOTS - 2, score_a, (head, SLOTS - 1), score_b)
        if follows:
            turn_queries(head + 1)
        step_over(SLOTS - 1, score_b, (head + 1, 0) if follows else None, score_a)

        sums_row = acc[SIZE : SIZE + 1, :]
        log_sum = peak[0:1, :] + jnp.log2(sums_row)
        whole = (acc[0:SIZE, :] * (1.0 / sums_row)).astype(BF16)
        whole = jnp.concatenate([whole, jnp.zeros((LANES - SIZE, columns), BF16)], axis=0)
        for slot in (1, 3, 2, 0):
            area = slice(slot * block, (slot + 1) * block)
            upright = whole[:, area].T[:, :SIZE]
            for d in range(SIDE):
                o_out[head, slot, d * FOLD : (d + 1) * FOLD] = fold(
                    upright[d * rows : (d + 1) * rows]
                )
            spare = l_out.shape[3] - block
            line = jnp.concatenate([log_sum[:, area], jnp.zeros((1, spare), F32)], axis=1)
            l_out[head, slot] = jnp.broadcast_to(line, l_out.shape[2:])
            if slot:
                to = x_to[SIDE - slot]
                o_x[head, slot] = send(
                    o_out.at[head, slot], o_in.at[head, slot - 1], o_send.at[head, slot - 1],
                    o_recv.at[head, slot - 1], to,
                )
                l_x[head, slot] = send(
                    l_out.at[head, slot], l_in.at[head, slot - 1], o_send.at[head, slot + 2],
                    o_recv.at[head, slot + 2], to,
                )

    def merge(head):
        for slot in ahead:
            o_x[head, slot].wait_recv()
            l_x[head, slot].wait_recv()
        logs = [l_out[head, 0, 0:1]] + [l_in[head, slot - 1, 0:1] for slot in ahead]
        top = functools.reduce(jnp.maximum, logs)
        shares = [jnp.exp2(log - top) for log in logs]
        inverse = 1.0 / functools.reduce(jnp.add, shares)
        shares = [share * inverse for share in shares]
        shares = jnp.concatenate(shares + shares, axis=0).T
        pieces = [o_out.at[head, 0]] + [o_in.at[head, slot - 1] for slot in ahead]
        return functools.reduce(
            jnp.add,
            [
                unfold(piece, rows).astype(F32) * shares[:block, i : i + 1]
                for i, piece in enumerate(pieces)
            ],
        )

    b_y = {}

    def give_back(tile, value):
        mine[tile] = value.astype(BF16)
        for d in ahead:
            b_y[tile, d] = send(
                mine.at[tile, pl.ds(d * rows, rows)], back.at[tile, d],
                b_send.at[tile, d - 1], b_recv.at[tile, d - 1], y_to[SIDE - d],
            )

    give_back(0, jnp.concatenate([merge(0), merge(1)], axis=1))
    give_back(1, jnp.concatenate([merge(2), jnp.zeros((block, SIZE), F32)], axis=1))
    mixed = hidden
    loads[4].wait()
    for tile in range(2):
        used = LANES if tile == 0 else SIZE
        for d in range(SIDE):
            if d:
                b_y[tile, d].wait_recv()
                piece = back[tile, d]
            else:
                piece = mine[tile, 0:rows]
            owner = lax.rem(y + d, SIDE)
            start = pl.multiple_of(owner * SHARE + tile * LANES, 16)
            mixed = mixed + jnp.dot(
                piece[:, :used], w_out[pl.ds(start, used), :], preferred_element_type=F32
            )
    resid = mixed.astype(BF16).astype(F32)
    normed = norm_rows(resid, gain_mlp[...][None, :])
    loads[5].wait()
    loads[6].wait()
    encoded = resid
    for at in range(0, w_up.shape[1], width):
        raised = jnp.dot(normed, w_up[:, at : at + width], preferred_element_type=F32)
        active = jax.nn.gelu(raised).astype(BF16)
        encoded = encoded + jnp.dot(active, w_down[at : at + width, :], preferred_element_type=F32)
    out_ref[...] = encoded.astype(BF16)
    for copy in copies:
        copy.wait_send()
    for head in range(TEAM):
        for slot, to in FORWARD.items():
            pltpu.make_async_copy(
                kv_all.at[head, slot], kv_all.at[head, slot], c_send.at[head, to]
            ).wait()


def on_device(tile_embeds, w_in, perturb, gain_attn, w_qkv, temper, w_out, gain_mlp, w_up, w_down):
    width = w_qkv.shape[0]
    rows = tile_embeds.shape[1] // GROUPS
    block = SIDE * rows
    columns = SIDE * block
    dma = pltpu.SemaphoreType.DMA
    vmem = pltpu.VMEM
    return pl.pallas_call(
        layer_kernel,
        out_shape=jax.ShapeDtypeStruct((rows, width), BF16),
        in_specs=[ANY, ANY, ANY, VMEM, ANY, SMEM, ANY, VMEM, ANY, ANY],
        out_specs=VMEM,
        scratch_shapes=[
            vmem(tile_embeds.shape, BF16), vmem(w_in.shape, BF16), vmem(perturb.shape, BF16),
            vmem(w_qkv.shape, BF16), vmem(w_out.shape, BF16), vmem(w_up.shape, BF16),
            vmem(w_down.shape, BF16),
            vmem((SIDE, 2, w_in.shape[0], width // 2), BF16),
            vmem((SIDE, 3 * rows, LANES), BF16),
            vmem((SIDE - 1, 3 * rows, LANES), BF16),
            vmem((2, rows, width // 2), BF16),
            vmem((2, rows, width // 2), BF16),
            vmem((TEAM, SIDE, FOLD, LANES), BF16),
            vmem((TEAM, SIDE, rows, LANES), BF16),
            vmem((TEAM, SIDE, SIDE * FOLD, LANES), BF16),
            vmem((TEAM, SLOTS, block, LANES), BF16),
            vmem((2, LANES, columns), BF16),
            vmem((block, columns), F32),
            vmem((block, columns), F32),
            vmem((SIZE + 8, columns), F32),
            vmem((8, columns), F32),
            vmem((TEAM, SIDE, SIDE * FOLD, LANES), BF16),
            vmem((TEAM, SIDE - 1, SIDE * FOLD, LANES), BF16),
            vmem((TEAM, SIDE, 8, 640), F32),
            vmem((TEAM, SIDE - 1, 8, 640), F32),
            vmem((2, block, LANES), BF16),
            vmem((2, SIDE, rows, LANES), BF16),
            dma((7,)), dma((5, 3)), dma((5, 3)), dma((2, 3)), dma((2, 3)), dma((2,)), dma((2,)),
            dma((6, 3)), dma((6, 3)), dma((TEAM, 3)), dma((TEAM, 3)),
            dma((TEAM, 3)), dma((TEAM, SLOTS)), dma((TEAM, SLOTS)),
            dma((TEAM, 6)), dma((TEAM, 6)), dma((2, 3)), dma((2, 3)),
        ],
        compiler_params=pltpu.CompilerParams(
            collective_id=0, has_side_effects=True, vmem_limit_bytes=56 * 2**20
        ),
        name="layer",
    )(tile_embeds, w_in, perturb, gain_attn, w_qkv, temper, w_out, gain_mlp, w_up, w_down)


def solution(mesh):
    placed = (P("grp", "seq"), P("grp", None), P("grp", None), P(), P(), P(), P(), P(), P(), P())
    return jax.shard_map(
        on_device, mesh=mesh, in_specs=placed, out_specs=P(("seq", "grp"), None), check_vma=False
    )
```
